256 devices in a mesh: dp: 16 (over z, x_hi), expert: 16 (over x_lo, y, core).
Axes of the slice: x: 4 (x_hi: 2, x_lo: 2; x = x_hi * 2 + x_lo), y: 4, z: 8, core: 2. Of those that a mesh axis runs over, the one named last changes fastest.
Arguments:
- acts: bfloat16 [16, 8192, 4096], P('expert', 'dp'), may hold values from -6 to 6
- out_grads: bfloat16 [16, 8192, 1024], P('expert', 'dp'), may hold values from -0.119628906 to 0.119628906
- master: float32 [16, 4096, 1024], P('expert', 'dp')
- moment_one: float32 [16, 4096, 1024], P('expert', 'dp'), may hold values from -6 to 6
- moment_two: float32 [16, 4096, 1024], P('expert', 'dp'), may hold values from 0.5 to 5
- routing: int32 [16, 16, 16], P('expert', 'dp'), may hold values from 0 to 15, each once within a row
- group_of: int32 [16], replicated, may hold values from 0 to 15, each once
Outputs:
- new_master: float32 [16, 4096, 1024], P('expert', 'dp')
- new_moment_one: float32 [16, 4096, 1024], P('expert', 'dp')
- new_moment_two: float32 [16, 4096, 1024], P('expert', 'dp')
- rollout_blocks: bfloat16 [16, 16, 16, 1, 128, 128], P('expert', 'dp')
- rollout_scales: bfloat16 [16, 16, 16, 1], P('expert', 'dp')
The draws below stay inside these ranges and needn't reach their ends.
Inputs may be any that keep to these rules, and one draw needn't show every extreme that they name: `routing`: each row is a permutation of the slots 0 to 15. `group_of`: a permutation of the expert groups.
All inputs are finite; a program needn't handle non-finite values. Where the reference program divides by a largest or mean magnitude, that divisor is 1e-20 or more.
Results may differ from the reference program's by a relative error of at most 0.0004.
The reference program's roundings to bfloat16 on the way (of `scale` and `quantized`) count: a program that leaves them out, or rounds other values in their place, can miss the bound.
Values may be sent and summed in bfloat16 or wider, within the bound.
A program may use at most 128 MiB of HBM per device.

```python
import math
import jax
import jax.numpy as jnp
from jax import lax

ROWS = 4096
COLS = 1024
BLOCK = 128
EXPERTS = 16
TOKENS = 8192
OWN_ROWS = 256
NBLOCKS = 16
PER_DEST = 1
N_DP = 16
N_EXPERT = 16


def draw_master(key, part):
    key = jax.random.fold_in(key, 7)
    key_base, key_rows, key_cols = jax.random.split(key, 3)
    base = jax.random.normal(key_base, (EXPERTS, ROWS, COLS), jnp.float32)
    spread = math.log(10.0)
    row_scale = jnp.exp(jax.random.uniform(key_rows, (EXPERTS, ROWS, 1), jnp.float32, 0.0, spread))
    col_scale = jnp.exp(jax.random.uniform(key_cols, (EXPERTS, 1, COLS), jnp.float32, 0.0, spread))
    return (0.001 * base * row_scale * col_scale).astype(jnp.float32)


def block_levels(stream_key, dims, shards, least, high):
    loudness, own = 1.0, jax.random.fold_in(stream_key, 6)
    for axis_at, shards_of in shards:
        steps = jnp.exp(jax.random.uniform(jax.random.fold_in(own, axis_at), (shards_of,), jnp.float32, least / len(shards), high / len(shards)))
        loudness = loudness * jnp.repeat(steps, dims[axis_at] // shards_of).reshape([-1 if axis == axis_at else 1 for axis in range(len(dims))])
    return loudness


def gaussian(rng, extent, scale, reach, cuts=(), kind=jnp.bfloat16):
    result = jax.random.normal(rng, extent, jnp.float32) * scale
    if len(cuts) > 0:
        result = block_levels(rng, extent, cuts, -0.22, 0.18) * result
    return jnp.clip(result, min=-reach, max=reach).astype(kind)


def setup_inputs(seed: int = 0) -> dict:
    seeds = jax.random.split(jax.random.key(seed), 8)
    return {
        "acts": gaussian(seeds[0], (EXPERTS, TOKENS, ROWS), 1.0, 6.0, ((0, 16), (1, 16))),
        "out_grads": gaussian(seeds[1], (EXPERTS, TOKENS, COLS), 0.02, 0.119628906, ((0, 16), (1, 16))),
        "master": draw_master(jax.random.fold_in(seeds[7], 71), 0),
        "moment_one": gaussian(seeds[3], (EXPERTS, ROWS, COLS), 1.0, 6.0, ((0, 16), (1, 16)), jnp.float32),
        "moment_two": jnp.clip(jnp.exp(math.log(5.0) - 2.3025851 * jax.random.uniform(seeds[4], (EXPERTS, ROWS, COLS), jnp.float32) ** block_levels(seeds[4], (EXPERTS, ROWS, COLS), ((0, 16), (1, 16)), -0.2, 0.2)), 0.5, 5.0),
        "routing": jax.vmap(lambda own: jax.random.permutation(own, NBLOCKS))(jax.random.split(seeds[5], EXPERTS * N_DP)).reshape((EXPERTS, N_DP, NBLOCKS)).astype(jnp.int32),
        "group_of": jax.random.permutation(seeds[6], EXPERTS).astype(jnp.int32),
    }


beta_one = 0.9
beta_two = 0.95
learn_rate = 0.01
decay_rate = 0.1
adam_eps = 1e-08
corr_one = 1.0 - 0.9 ** 10
corr_two = 1.0 - 0.95 ** 10

def reference(acts, out_grads, master, moment_one, moment_two, routing, group_of):
    expert_of = jnp.argsort(group_of).astype(jnp.int32)
    per_row = OWN_ROWS // BLOCK
    per_col = COLS // BLOCK
    masters, firsts, seconds = ([], [], [])
    blocks_out = jnp.zeros((N_EXPERT, N_DP, EXPERTS, PER_DEST, BLOCK, BLOCK), jnp.bfloat16)
    scales_out = jnp.zeros((N_EXPERT, N_DP, EXPERTS, PER_DEST), jnp.bfloat16)
    for group in range(EXPERTS):
        grad = lax.dot_general(acts[group], out_grads[group], (((0,), (0,)), ((), ())), preferred_element_type=jnp.float32)
        first = beta_one * moment_one[group] + (1.0 - beta_one) * grad
        second = beta_two * moment_two[group] + (1.0 - beta_two) * grad * grad
        weight = master[group]
        update = first / corr_one / (jnp.sqrt(second / corr_two) + adam_eps) + decay_rate * weight
        weight = weight - learn_rate * update
        masters.append(weight)
        firsts.append(first)
        seconds.append(second)
        tiles = weight.reshape(N_DP, per_row, BLOCK, per_col, BLOCK).transpose(0, 1, 3, 2, 4)
        tiles = tiles.reshape(N_DP, NBLOCKS, BLOCK, BLOCK)
        scale = (lax.optimization_barrier(jnp.max(jnp.abs(tiles), axis=(2, 3))) + 1e-06).astype(jnp.bfloat16)
        quantized = (tiles / scale.astype(jnp.float32)[:, :, None, None]).astype(jnp.bfloat16)
        slots = routing[group]
        owners = jnp.broadcast_to(jnp.arange(N_DP, dtype=jnp.int32)[:, None], slots.shape)
        target = slots // PER_DEST
        place = slots % PER_DEST
        ident = jnp.broadcast_to(expert_of[group], slots.shape)
        blocks_out = blocks_out.at[target, owners, ident, place].set(quantized)
        scales_out = scales_out.at[target, owners, ident, place].set(scale)
    return (jnp.stack(masters), jnp.stack(firsts), jnp.stack(seconds), blocks_out, scales_out)
```

```python
import math

import jax
import jax.numpy as jnp
from jax import lax
from jax.experimental import pallas as pl
from jax.experimental.pallas import tpu as pltpu
from jax.sharding import PartitionSpec as P

MESH = pl.DeviceIdType.MESH
BLOCK = 128
NZ = 8
ND = 16
NE = 16
OWN = 256
UC = 256
MSG = 2 * OWN + 16
LEVELS = 32766.0
FINE = 8.0
LN2 = math.log(2.0)

beta_one = 0.9
beta_two = 0.95
learn_rate = 0.01
decay_rate = 0.1
adam_eps = 1e-08
corr_one = 1.0 - 0.9**10
corr_two = 1.0 - 0.95**10


def encode(ref, halves):
    steps = []
    for h, v in enumerate(halves):
        top = jnp.max(jnp.abs(v), axis=0, keepdims=True)
        step = jnp.ceil(jnp.log(jnp.maximum(top, 2.0**-100)) * (FINE / LN2))
        inv = jnp.exp(step * (-LN2 / FINE)) * LEVELS
        ref[h * OWN : (h + 1) * OWN, :] = jnp.round(v * inv).astype(jnp.int32).astype(jnp.int16)
        steps.append(jnp.broadcast_to(step, (8, BLOCK)))
    ref[2 * OWN :, :] = jnp.concatenate(steps, axis=0).astype(jnp.int32).astype(jnp.int16)


def decode(ref):
    steps = ref[2 * OWN :, :].astype(jnp.int32).astype(jnp.float32)
    scales = jnp.exp(steps * (LN2 / FINE)) * (1.0 / LEVELS)
    return [
        ref[h * OWN : (h + 1) * OWN, :].astype(jnp.int32).astype(jnp.float32)
        * scales[8 * h : 8 * h + 1, :]
        for h in range(2)
    ]


def kernel(
    acts, grads, master, moment_one, moment_two, routing, group_of,
    master_out, one_out, two_out, blocks_out, scales_out,
    a_v, g_v, w_v, m_v, v_v, wt_v, mo_v, vo_v,
    s1_send, s1_recv, s2_send, s2_recv, x2_send, x2_recv, x1_send, x1_recv, ask, asked, reply, replied,
    stat_v, sel_v, place_v, answer_v, scale_v, r_send, r_recv,
    a_sem, in_sem, out_sem,
    s1_ss, s1_rs, s2_ss, s2_rs, x2_ss, x2_rs, x1_ss, x1_rs, ask_ss, ask_rs, rep_ss, rep_rs, r_ss, r_rs,
):
    dp = lax.axis_index("dp")
    ex = lax.axis_index("expert")
    z, xh = dp // 2, dp % 2

    def zdev(way):
        return (lax.rem(z + 1 + 6 * way, NZ) * 2 + xh, ex)

    partner = (z * 2 + 1 - xh, ex)
    mine = z * 2 + xh

    def load_acts(off, half):
        i = lax.rem(z + off, NZ) * 2 + half
        return pltpu.make_async_copy(
            acts.at[0, :, pl.ds(pl.multiple_of(i * OWN, OWN), OWN)], a_v.at[i], a_sem.at[i]
        )

    grads_copy = pltpu.make_async_copy(grads.at[0], g_v, in_sem.at[0])
    load_acts(4, 0).start()
    grads_copy.start()
    load_acts(4, 1).start()
    order = (3, 5, 2, 6, 1, 7, 0)
    for off in order:
        for half in range(2):
            load_acts(off, half).start()
    state = [
        pltpu.make_async_copy(src.at[0], dst, in_sem.at[1 + i])
        for i, (src, dst) in enumerate(((master, w_v), (moment_one, m_v), (moment_two, v_v)))
    ]
    for c in state:
        c.start()

    barrier = pltpu.get_barrier_semaphore()

    @pl.loop(1, NE)
    def _(k):
        pl.semaphore_signal(barrier, inc=1, device_id=(lax.rem(dp + k, ND), ex), device_id_type=MESH)
        pl.semaphore_signal(barrier, inc=1, device_id=(dp, lax.rem(ex + k, NE)), device_id_type=MESH)

    pl.semaphore_wait(barrier, ND - 1 + NE - 1)

    def partial(i, c):
        p = lax.dot_general(
            a_v[i],
            g_v[:, pl.ds(pl.multiple_of(c * UC, UC), UC)],
            (((0,), (0,)), ((), ())),
            preferred_element_type=jnp.float32,
        )
        return [p[:, :BLOCK], p[:, BLOCK:]]

    def add(a, b):
        return [u + v for u, v in zip(a, b)]

    def s1_copy(way, s, u):
        return pltpu.make_async_remote_copy(
            src_ref=s1_send.at[way, s, u], dst_ref=s1_recv.at[way, s, u],
            send_sem=s1_ss.at[way, s, u], recv_sem=s1_rs.at[way, s, u],
            device_id=zdev(way), device_id_type=MESH,
        )

    def s2_copy(way, s, c):
        return pltpu.make_async_remote_copy(
            src_ref=s2_send.at[way, s, c], dst_ref=s2_recv.at[way, s, c],
            send_sem=s2_ss.at[way, s, c], recv_sem=s2_rs.at[way, s, c],
            device_id=zdev(way), device_id_type=MESH,
        )

    def x2_copy(j):
        return pltpu.make_async_remote_copy(
            src_ref=x2_send.at[j], dst_ref=x2_recv.at[j],
            send_sem=x2_ss.at[j], recv_sem=x2_rs.at[j],
            device_id=partner, device_id_type=MESH,
        )

    def x1_copy(c):
        return pltpu.make_async_remote_copy(
            src_ref=x1_send.at[c], dst_ref=x1_recv.at[c],
            send_sem=x1_ss.at[c], recv_sem=x1_rs.at[c],
            device_id=partner, device_id_type=MESH,
        )

    def target(way, s):
        return lax.rem(z + 4 + (1 - 2 * way) * (-s) + NZ, NZ)

    def s1_task(way, s, u, arrived):
        v = partial(target(way, s) * 2 + u // 2, u % 2)
        if arrived:
            s1_copy(way, s - 1, u).wait_recv()
            v = add(v, decode(s1_recv.at[way, s - 1, u]))
        encode(s1_send.at[way, s, u], v)
        s1_copy(way, s, u).start()

    def x2_task(j):
        o = j // 2
        off = lax.select(o % 2 == 1, 4 - (o + 1) // 2, 4 + o // 2)
        encode(x2_send.at[j], partial(lax.rem(z + off, NZ) * 2 + 1 - xh, 2 + j % 2))
        x2_copy(j).start()

    def s2_task(way, s, c, arrived):
        v = partial(target(way, s) * 2 + xh, 2 + c)
        j = c if s == 0 else (2 * s - 1 + way) * 2 + c
        x2_copy(j).wait_recv()
        v = add(v, decode(x2_recv.at[j]))
        if arrived:
            s2_copy(way, s - 1, c).wait_recv()
            v = add(v, decode(s2_recv.at[way, s - 1, c]))
        encode(s2_send.at[way, s, c], v)
        s2_copy(way, s, c).start()

    load_acts(4, 0).wait()
    grads_copy.wait()
    load_acts(4, 1).wait()

    @pl.loop(0, 2)
    def _(k):
        s1_task(0, 0, k, False)
        s1_task(1, 0, 2 + k, False)
        x2_task(k)

    for off in order:
        for half in range(2):
            load_acts(off, half).wait()

    @pl.loop(2, 6)
    def _(j):
        x2_task(j)

    @pl.loop(0, 4)
    def _(k):
        way = k % 2
        s1_task(way, 1, 2 * (1 - way) + k // 2, False)
        s1_task(way, 1, 2 * way + k // 2, True)
        x2_task(6 + k)

    @pl.loop(0, 2)
    def _(way):
        s2_task(way, 0, way, False)

    @pl.loop(0, 4)
    def _(k):
        s1_task(0, 2, k, True)
        s1_task(1, 2, k, True)
        x2_task(10 + k)

    @pl.loop(0, 2)
    def _(way):
        s2_task(way, 1, 1 - way, False)
        s2_task(way, 1, way, True)

    @pl.loop(0, 4)
    def _(k):
        s2_task(k % 2, 2, k // 2, True)
        s1_task(0, 3, k, True)
        s1_task(1, 3, k, True)

    @pl.loop(0, 2)
    def _(c):
        x2_task(14 + c)

    @pl.loop(0, 4)
    def _(k):
        s2_task(k % 2, 3, k // 2, True)

    def s1_sum(half, c):
        u = 2 * half + c
        v = partial(z * 2 + half, c)
        for way in range(2):
            s1_copy(way, 3, u).wait_recv()
            v = add(v, decode(s1_recv.at[way, 3, u]))
        return v

    @pl.loop(0, 2)
    def _(c):
        encode(x1_send.at[c], s1_sum(1 - xh, c))
        x1_copy(c).start()

    for c in state:
        c.wait()

    def results(c):
        copies = []
        cols = pl.ds(pl.multiple_of(c * UC, UC), UC)
        for n, (src, dst) in enumerate(((mo_v, one_out), (vo_v, two_out))):
            copies.append(
                pltpu.make_async_copy(src.at[:, cols], dst.at[0, :, cols], out_sem.at[c, n])
            )
        for r in range(2):
            for h in range(2):
                b = r * 8 + 2 * c + h
                lanes = pl.ds(pl.multiple_of(c * UC + h * BLOCK, BLOCK), BLOCK)
                copies.append(
                    pltpu.make_async_copy(
                        wt_v.at[b],
                        master_out.at[0, pl.ds(r * BLOCK, BLOCK), lanes],
                        out_sem.at[c, 2 + 2 * r + h],
                    )
                )
        return copies

    def adam(weight, one, two, grad):
        first = beta_one * one + (1.0 - beta_one) * grad
        second = beta_two * two + (1.0 - beta_two) * grad * grad
        update = (first * (1.0 / corr_one)) / (
            jnp.sqrt(second * (1.0 / corr_two)) + adam_eps
        ) + decay_rate * weight
        return weight - learn_rate * update, first, second

    row_ids = lax.broadcasted_iota(jnp.int32, (BLOCK, BLOCK), 0)

    def finish(c, halves):
        for h, grad in enumerate(halves):
            cols = pl.ds(pl.multiple_of(c * UC + h * BLOCK, BLOCK), BLOCK)
            weight, first, second = adam(w_v[:, cols], m_v[:, cols], v_v[:, cols], grad)
            mo_v[:, cols] = first
            vo_v[:, cols] = second
            for r in range(2):
                b = r * 8 + 2 * c + h
                rows = slice(r * BLOCK, (r + 1) * BLOCK)
                tile = weight[rows, :]
                wt_v[b] = tile
                size = jnp.abs(tile)
                top = jnp.max(size, axis=0, keepdims=True)
                at = jnp.min(jnp.where(size == top, row_ids, BLOCK), axis=0, keepdims=True)
                one_row = row_ids == at
                stat_v[0, pl.ds(b, 1), :] = top
                stat_v[1, pl.ds(b, 1), :] = at.astype(jnp.float32)
                for n, src in enumerate((w_v, m_v, v_v)):
                    stat_v[2 + n, pl.ds(b, 1), :] = jnp.sum(
                        jnp.where(one_row, src[rows, cols], 0.0), axis=0, keepdims=True
                    )
        for copy in results(c):
            copy.start()

    @pl.loop(0, 2)
    def _(c):
        v = s1_sum(xh, c)
        x1_copy(c).wait_recv()
        finish(c, add(v, decode(x1_recv.at[c])))

    @pl.loop(0, 2)
    def _(c):
        v = partial(mine, 2 + c)
        x2_copy(14 + c).wait_recv()
        v = add(v, decode(x2_recv.at[14 + c]))
        for way in range(2):
            s2_copy(way, 3, c).wait_recv()
            v = add(v, decode(s2_recv.at[way, 3, c]))
        finish(2 + c, v)

    def ask_copy(peer, source):
        return pltpu.make_async_remote_copy(
            src_ref=ask, dst_ref=asked.at[source],
            send_sem=ask_ss.at[peer], recv_sem=ask_rs.at[source],
            device_id=(peer, ex), device_id_type=MESH,
        )

    def reply_copy(peer, source):
        return pltpu.make_async_remote_copy(
            src_ref=reply.at[peer // 8], dst_ref=replied.at[source],
            send_sem=rep_ss.at[peer], recv_sem=rep_rs.at[source],
            device_id=(peer, ex), device_id_type=MESH,
        )

    lanes = lax.broadcasted_iota(jnp.int32, (NE, BLOCK), 1)
    blocks = lax.broadcasted_iota(jnp.int32, (NE, BLOCK), 0)
    slots = lanes == lax.rem(dp, 8) * NE + blocks
    top = stat_v[0]
    most = jnp.max(top, axis=1, keepdims=True)
    lane = jnp.min(jnp.where(top == most, lanes, BLOCK), axis=1, keepdims=True)
    here = lanes == lane

    def along(x):
        return jnp.sum(jnp.where(slots, x, 0.0), axis=0, keepdims=True)

    picked = [jnp.sum(jnp.where(here, stat_v[n], 0.0), axis=1, keepdims=True) for n in range(1, 5)]
    col_at = along((blocks % 8 * BLOCK + lane).astype(jnp.float32))
    row_at = along((blocks // 8 * BLOCK).astype(jnp.float32) + picked[0])
    ask[...] = jnp.concatenate(
        [jnp.broadcast_to(row_at, (8, BLOCK)), jnp.broadcast_to(col_at, (8, BLOCK))], axis=0
    )

    @pl.loop(1, ND)
    def _(k):
        ask_copy(lax.rem(dp + k, ND), dp).start()

    asked[dp] = ask[...]
    old = [along(x) for x in picked[1:]]

    @pl.loop(1, ND)
    def _(k):
        source = lax.rem(dp + k, ND)
        ask_copy(source, source).wait_recv()

    for half in range(2):
        total = asked[8 * half]
        for n in range(1, 8):
            total = total + asked[8 * half + n]
        rows = total[0:1, :].astype(jnp.int32)
        cols = total[8:9, :].astype(jnp.int32)
        place_v[half] = (
            lax.broadcasted_iota(jnp.int32, (OWN, BLOCK), 0) == rows
        ).astype(jnp.float32).astype(jnp.bfloat16)
        sel_v[half] = jnp.dot(
            g_v[...],
            (lax.broadcasted_iota(jnp.int32, (g_v.shape[1], BLOCK), 0) == cols)
            .astype(jnp.float32)
            .astype(jnp.bfloat16),
            preferred_element_type=jnp.float32,
        )
    answer_v[...] = jnp.zeros_like(answer_v)
    groups = lax.broadcasted_iota(jnp.int32, (8, BLOCK), 1) // NE

    @pl.loop(0, ND)
    def _(o):
        half = o // 8
        chosen = jnp.dot(a_v[o], place_v[half], preferred_element_type=jnp.float32)
        dots = jnp.sum(chosen * sel_v[half], axis=0, keepdims=True)
        answer_v[half] = jnp.where(groups == lax.rem(o, 8), dots, answer_v[half])

    reply[...] = answer_v[...]

    @pl.loop(1, ND)
    def _(k):
        reply_copy(lax.rem(dp + k, ND), dp).start()

    replied[dp] = answer_v[dp // 8]

    @pl.loop(1, ND)
    def _(k):
        source = lax.rem(dp + k, ND)
        reply_copy(source, source).wait_recv()

    exact = replied[0]
    for n in range(1, ND):
        exact = exact + replied[n]
    largest = jnp.abs(adam(*old, exact[0:1, :])[0])
    scale = (largest + 1e-06).astype(jnp.bfloat16).astype(jnp.float32)
    scale = jnp.sum(jnp.where(slots, scale, 0.0), axis=1, keepdims=True)
    for b in range(NE):
        scale_v[b] = jnp.broadcast_to(scale[b : b + 1, :], (8, BLOCK))

    def roll_copy(slot, source):
        return pltpu.make_async_remote_copy(
            src_ref=r_send.at[slot], dst_ref=r_recv.at[source],
            send_sem=r_ss.at[slot], recv_sem=r_rs.at[source],
            device_id=(dp, slot), device_id_type=MESH,
        )

    def held(slot):
        b = jnp.int32(0)
        for n in range(NE):
            b = lax.select(routing[0, 0, n] == slot, jnp.int32(n), b)
        return b

    def pack(ref, b):
        wide = scale_v[b]
        ref[:BLOCK, :] = (wt_v[b] / wide[0:1, :]).astype(jnp.bfloat16)
        ref[BLOCK:, :] = jnp.broadcast_to(wide[0:1, :], (16, BLOCK)).astype(jnp.bfloat16)

    @pl.loop(1, NE)
    def _(k):
        slot = lax.rem(ex + k, NE)
        pack(r_send.at[slot], held(slot))
        roll_copy(slot, ex).start()

    pack(r_recv.at[ex], held(ex))

    @pl.loop(1, NE)
    def _(k):
        source = lax.rem(ex + k, NE)
        roll_copy(source, source).wait_recv()

    for e in range(NE):
        block = r_recv[group_of[e]]
        blocks_out[e] = block[:BLOCK, :]
        scales_out[e] = block[BLOCK:, :]

    @pl.loop(1, NE)
    def _(k):
        slot = lax.rem(ex + k, NE)
        roll_copy(slot, ex).wait_send()
        peer = lax.rem(dp + k, ND)
        ask_copy(peer, dp).wait_send()
        reply_copy(peer, dp).wait_send()

    @pl.loop(0, 2)
    def _(way):
        for n in range(2):
            s1_copy(way, 0, 2 * way + n).wait_send()
        s2_copy(way, 0, way).wait_send()
        x1_copy(way).wait_send()

        @pl.loop(1, 4)
        def _(s):
            for u in range(4):
                s1_copy(way, s, u).wait_send()
            for c in range(2):
                s2_copy(way, s, c).wait_send()

    @pl.loop(0, 2 * NZ)
    def _(j):
        x2_copy(j).wait_send()

    for c in range(4):
        for copy in results(c):
            copy.wait()


def per_device(acts, out_grads, master, moment_one, moment_two, routing, group_of):
    f32, i16, bf16 = jnp.float32, jnp.int16, jnp.bfloat16
    own, width = master.shape[1], master.shape[2]
    tokens = acts.shape[1]
    dma = pltpu.SemaphoreType.DMA
    hbm = pl.BlockSpec(memory_space=pl.ANY)
    smem = pl.BlockSpec(memory_space=pltpu.SMEM)
    vmem = pl.BlockSpec(memory_space=pltpu.VMEM)
    shape = jax.ShapeDtypeStruct
    weight, first, second, blocks, scales = pl.pallas_call(
        kernel,
        out_shape=(
            shape((1, own, width), f32),
            shape((1, own, width), f32),
            shape((1, own, width), f32),
            shape((NE, BLOCK, BLOCK), bf16),
            shape((NE, 16, BLOCK), bf16),
        ),
        in_specs=[hbm] * 5 + [smem] * 2,
        out_specs=(hbm, hbm, hbm, vmem, vmem),
        scratch_shapes=[
            pltpu.VMEM((2 * NZ, tokens, OWN), bf16),
            pltpu.VMEM((tokens, width), bf16),
            pltpu.VMEM((own, width), f32),
            pltpu.VMEM((own, width), f32),
            pltpu.VMEM((own, width), f32),
            pltpu.VMEM((NE, BLOCK, BLOCK), f32),
            pltpu.VMEM((own, width), f32),
            pltpu.VMEM((own, width), f32),
            pltpu.VMEM((2, 4, 4, MSG, BLOCK), i16),
            pltpu.VMEM((2, 4, 4, MSG, BLOCK), i16),
            pltpu.VMEM((2, 4, 2, MSG, BLOCK), i16),
            pltpu.VMEM((2, 4, 2, MSG, BLOCK), i16),
            pltpu.VMEM((2 * NZ, MSG, BLOCK), i16),
            pltpu.VMEM((2 * NZ, MSG, BLOCK), i16),
            pltpu.VMEM((2, MSG, BLOCK), i16),
            pltpu.VMEM((2, MSG, BLOCK), i16),
            pltpu.VMEM((16, BLOCK), f32),
            pltpu.VMEM((ND, 16, BLOCK), f32),
            pltpu.VMEM((2, 8, BLOCK), f32),
            pltpu.VMEM((ND, 8, BLOCK), f32),
            pltpu.VMEM((5, NE, BLOCK), f32),
            pltpu.VMEM((2, tokens, BLOCK), f32),
            pltpu.VMEM((2, own, BLOCK), bf16),
            pltpu.VMEM((2, 8, BLOCK), f32),
            pltpu.VMEM((NE, 8, BLOCK), f32),
            pltpu.VMEM((NE, BLOCK + 16, BLOCK), bf16),
            pltpu.VMEM((NE, BLOCK + 16, BLOCK), bf16),
            dma((2 * NZ,)),
            dma((4,)),
            dma((4, 6)),
            dma((2, 4, 4)),
            dma((2, 4, 4)),
            dma((2, 4, 2)),
            dma((2, 4, 2)),
            dma((2 * NZ,)),
            dma((2 * NZ,)),
            dma((2,)),
            dma((2,)),
            dma((ND,)),
            dma((ND,)),
            dma((ND,)),
            dma((ND,)),
            dma((NE,)),
            dma((NE,)),
        ],
        name="update",
        cost_estimate=pl.CostEstimate(
            flops=2 * tokens * acts.shape[2] * width, bytes_accessed=12 * 2**20, transcendentals=0
        ),
        compiler_params=pltpu.CompilerParams(
            collective_id=0, has_side_effects=True, vmem_limit_bytes=56 * 2**20
        ),
    )(acts, out_grads, master, moment_one, moment_two, routing, group_of)
    return (
        weight,
        first,
        second,
        blocks.reshape(1, 1, NE, 1, BLOCK, BLOCK),
        scales[:, 0, 0].reshape(1, 1, NE, 1),
    )


def solution(mesh):
    in_specs = (P("expert", "dp", None),) * 6 + (P(),)
    out_specs = (
        P("expert", "dp", None),
        P("expert", "dp", None),
        P("expert", "dp", None),
        P("expert", "dp", None, None, None, None),
        P("expert", "dp", None, None),
    )
    return jax.shard_map(
        per_device, mesh=mesh, in_specs=in_specs, out_specs=out_specs, check_vma=False
    )
```

```python
import math

import jax
import jax.numpy as jnp
from jax import lax
from jax.experimental import pallas as pl
from jax.experimental.pallas import tpu as pltpu
from jax.sharding import PartitionSpec as P

MESH = pl.DeviceIdType.MESH
BLOCK = 128
NZ = 8
ND = 16
NE = 16
OWN = 256
UC = 256
MSG = 2 * OWN + 16
LEVELS = 32766.0
FINE = 8.0
LN2 = math.log(2.0)

beta_one = 0.9
beta_two = 0.95
learn_rate = 0.01
decay_rate = 0.1
adam_eps = 1e-08
corr_one = 1.0 - 0.9**10
corr_two = 1.0 - 0.95**10

ORDER = (
    0, 18, 128, 1, 19, 129, 20, 130, 141, 6, 21, 134, 7, 86,
    68, 69, 87, 132, 133, 89, 192, 209, 74, 88, 73, 131, 138, 139,
    75, 135, 212, 91, 72, 277, 90, 260, 78, 136, 79, 137, 77, 93,
    197, 142, 143, 95, 92, 140, 264, 76, 280, 94, 321, 265, 281, 284,
    268, 320, 269, 285, 384, 448, 385, 449,
)
HEAD = 6


def pick(k, values):
    if len(set(values)) == 1:
        return jnp.int32(values[0])
    half = len(values) // 2
    return lax.select(k < half, pick(k, values[:half]), pick(k - half, values[half:]))


def adam(weight, one, two, grad):
    first = beta_one * one + (1.0 - beta_one) * grad
    second = beta_two * two + (1.0 - beta_two) * grad * grad
    update = first / corr_one / (jnp.sqrt(second / corr_two) + adam_eps) + decay_rate * weight
    return weight - learn_rate * update, first, second


def encode(ref, halves):
    steps = []
    for h, v in enumerate(halves):
        top = jnp.max(jnp.abs(v), axis=0, keepdims=True)
        step = jnp.ceil(jnp.log(jnp.maximum(top, 2.0**-100)) * (FINE / LN2))
        inv = jnp.exp(step * (-LN2 / FINE)) * LEVELS
        ref[h * OWN : (h + 1) * OWN, :] = jnp.round(v * inv).astype(jnp.int32).astype(jnp.int16)
        steps.append(jnp.broadcast_to(step, (8, BLOCK)))
    ref[2 * OWN :, :] = jnp.concatenate(steps, axis=0).astype(jnp.int32).astype(jnp.int16)


def decode(ref):
    steps = ref[2 * OWN :, :].astype(jnp.int32).astype(jnp.float32)
    scales = jnp.exp(steps * (LN2 / FINE)) * (1.0 / LEVELS)
    return [
        ref[h * OWN : (h + 1) * OWN, :].astype(jnp.int32).astype(jnp.float32)
        * scales[8 * h : 8 * h + 1, :]
        for h in range(2)
    ]


def kernel(
    acts, grads, master, moment_one, moment_two, routing, group_of,
    grad_out, blocks_out, scales_out,
    a_v, g_v, w_v, m_v, v_v, wt_v, sum_v,
    s1_send, s1_recv, s2_send, s2_recv, x2_send, x2_recv, x1_send, x1_recv, ask, asked, reply, replied,
    stat_v, sel_v, place_v, answer_v, scale_v, r_send, r_recv,
    a_sem, in_sem, out_sem,
    s1_ss, s1_rs, s2_ss, s2_rs, x2_ss, x2_rs, x1_ss, x1_rs, ask_ss, ask_rs, rep_ss, rep_rs, r_ss, r_rs,
):
    dp = lax.axis_index("dp")
    ex = lax.axis_index("expert")
    z, xh = dp // 2, dp % 2

    def zdev(way):
        return (lax.rem(z + 1 + 6 * way, NZ) * 2 + xh, ex)

    partner = (z * 2 + 1 - xh, ex)
    mine = z * 2 + xh

    def load_acts(off, half):
        i = lax.rem(z + off, NZ) * 2 + half
        return pltpu.make_async_copy(
            acts.at[0, :, pl.ds(pl.multiple_of(i * OWN, OWN), OWN)], a_v.at[i], a_sem.at[i]
        )

    grads_copy = pltpu.make_async_copy(grads.at[0], g_v, in_sem.at[0])
    load_acts(4, 0).start()
    grads_copy.start()
    load_acts(4, 1).start()
    order = (3, 5, 2, 6, 1, 7, 0)
    for off in order:
        for half in range(2):
            load_acts(off, half).start()
    state = [
        pltpu.make_async_copy(src.at[0], dst, in_sem.at[1 + i])
        for i, (src, dst) in enumerate(((master, w_v), (moment_one, m_v), (moment_two, v_v)))
    ]
    for c in state:
        c.start()

    barrier = pltpu.get_barrier_semaphore()

    @pl.loop(1, NE)
    def _(k):
        pl.semaphore_signal(barrier, inc=1, device_id=(lax.rem(dp + k, ND), ex), device_id_type=MESH)
        pl.semaphore_signal(barrier, inc=1, device_id=(dp, lax.rem(ex + k, NE)), device_id_type=MESH)

    pl.semaphore_wait(barrier, ND - 1 + NE - 1)

    def partial(i, c):
        p = lax.dot_general(
            a_v[i],
            g_v[:, pl.ds(pl.multiple_of(c * UC, UC), UC)],
            (((0,), (0,)), ((), ())),
            preferred_element_type=jnp.float32,
        )
        return [p[:, :BLOCK], p[:, BLOCK:]]

    def add(a, b):
        return [u + v for u, v in zip(a, b)]

    def s1_copy(way, s, u):
        return pltpu.make_async_remote_copy(
            src_ref=s1_send.at[way, s, u], dst_ref=s1_recv.at[way, s, u],
            send_sem=s1_ss.at[way, s, u], recv_sem=s1_rs.at[way, s, u],
            device_id=zdev(way), device_id_type=MESH,
        )

    def s2_copy(way, s, c):
        return pltpu.make_async_remote_copy(
            src_ref=s2_send.at[way, s, c], dst_ref=s2_recv.at[way, s, c],
            send_sem=s2_ss.at[way, s, c], recv_sem=s2_rs.at[way, s, c],
            device_id=zdev(way), device_id_type=MESH,
        )

    def x2_copy(j):
        return pltpu.make_async_remote_copy(
            src_ref=x2_send.at[j], dst_ref=x2_recv.at[j],
            send_sem=x2_ss.at[j], recv_sem=x2_rs.at[j],
            device_id=partner, device_id_type=MESH,
        )

    def x1_copy(c):
        return pltpu.make_async_remote_copy(
            src_ref=x1_send.at[c], dst_ref=x1_recv.at[c],
            send_sem=x1_ss.at[c], recv_sem=x1_rs.at[c],
            device_id=partner, device_id_type=MESH,
        )

    def target(way, s):
        return lax.rem(z + 4 + (1 - 2 * way) * (-s) + NZ, NZ)

    def s1_task(way, s, u, arrived):
        v = partial(target(way, s) * 2 + u // 2, u % 2)
        if arrived:
            s1_copy(way, s - 1, u).wait_recv()
            v = add(v, decode(s1_recv.at[way, s - 1, u]))
        encode(s1_send.at[way, s, u], v)
        s1_copy(way, s, u).start()

    def x2_task(j):
        o = j // 2
        off = lax.select(o % 2 == 1, 4 - (o + 1) // 2, 4 + o // 2)
        encode(x2_send.at[j], partial(lax.rem(z + off, NZ) * 2 + 1 - xh, 2 + j % 2))
        x2_copy(j).start()

    def s2_task(way, s, c, arrived):
        v = partial(target(way, s) * 2 + xh, 2 + c)
        j = lax.select(s == 0, c, (2 * s - 1 + way) * 2 + c)
        x2_copy(j).wait_recv()
        v = add(v, decode(x2_recv.at[j]))
        if arrived:
            s2_copy(way, s - 1, c).wait_recv()
            v = add(v, decode(s2_recv.at[way, s - 1, c]))
        encode(s2_send.at[way, s, c], v)
        s2_copy(way, s, c).start()

    def s1_sum(half, c):
        u = 2 * half + c
        v = partial(z * 2 + half, c)
        for way in range(2):
            s1_copy(way, 3, u).wait_recv()
            v = add(v, decode(s1_recv.at[way, 3, u]))
        return v

    def result(c):
        cols = pl.ds(pl.multiple_of(c * UC, UC), UC)
        return pltpu.make_async_copy(sum_v.at[:, cols], grad_out.at[:, cols], out_sem.at[c])

    row_ids = lax.broadcasted_iota(jnp.int32, (BLOCK, BLOCK), 0)

    def finish(c, halves):
        for h, grad in enumerate(halves):
            cols = pl.ds(pl.multiple_of(c * UC + h * BLOCK, BLOCK), BLOCK)
            sum_v[:, cols] = grad
            weight = adam(w_v[:, cols], m_v[:, cols], v_v[:, cols], grad)[0]
            for r in range(2):
                b = r * 8 + 2 * c + h
                rows = slice(r * BLOCK, (r + 1) * BLOCK)
                tile = weight[rows, :]
                wt_v[b] = tile
                size = jnp.abs(tile)
                top = jnp.max(size, axis=0, keepdims=True)
                at = jnp.min(jnp.where(size == top, row_ids, BLOCK), axis=0, keepdims=True)
                one_row = row_ids == at
                stat_v[0, pl.ds(b, 1), :] = top
                stat_v[1, pl.ds(b, 1), :] = at.astype(jnp.float32)
                for n, src in enumerate((w_v, m_v, v_v)):
                    stat_v[2 + n, pl.ds(b, 1), :] = jnp.sum(
                        jnp.where(one_row, src[rows, cols], 0.0), axis=0, keepdims=True
                    )
        result(c).start()

    def x1_task(c):
        encode(x1_send.at[c], s1_sum(1 - xh, c))
        x1_copy(c).start()

    def finish_s1(c):
        v = s1_sum(xh, c)
        x1_copy(c).wait_recv()
        finish(c, add(v, decode(x1_recv.at[c])))

    def finish_s2(c):
        v = partial(mine, 2 + c)
        x2_copy(14 + c).wait_recv()
        v = add(v, decode(x2_recv.at[14 + c]))
        for way in range(2):
            s2_copy(way, 3, c).wait_recv()
            v = add(v, decode(s2_recv.at[way, 3, c]))
        finish(2 + c, v)

    load_acts(4, 0).wait()
    grads_copy.wait()
    load_acts(4, 1).wait()

    @pl.loop(0, len(ORDER))
    def _(k):
        @pl.when(k == HEAD)
        def _():
            for off in order:
                for half in range(2):
                    load_acts(off, half).wait()
            for c in state:
                c.wait()

        code = pick(k, ORDER)
        kind = code // 64
        way, s, u = code // 16 % 4, code // 4 % 4, code % 4
        for n, task in enumerate(
            (
                lambda: s1_task(way, s, u, False),
                lambda: s1_task(way, s, u, True),
                lambda: x2_task(code % 64),
                lambda: s2_task(way, s, u, False),
                lambda: s2_task(way, s, u, True),
                lambda: x1_task(u),
                lambda: finish_s1(u),
                lambda: finish_s2(u),
            )
        ):
            pl.when(kind == n)(task)

    def ask_copy(peer, source):
        return pltpu.make_async_remote_copy(
            src_ref=ask, dst_ref=asked.at[source],
            send_sem=ask_ss.at[peer], recv_sem=ask_rs.at[source],
            device_id=(peer, ex), device_id_type=MESH,
        )

    def reply_copy(peer, source):
        return pltpu.make_async_remote_copy(
            src_ref=reply.at[peer // 8], dst_ref=replied.at[source],
            send_sem=rep_ss.at[peer], recv_sem=rep_rs.at[source],
            device_id=(peer, ex), device_id_type=MESH,
        )

    lanes = lax.broadcasted_iota(jnp.int32, (NE, BLOCK), 1)
    blocks = lax.broadcasted_iota(jnp.int32, (NE, BLOCK), 0)
    slots = lanes == lax.rem(dp, 8) * NE + blocks
    top = stat_v[0]
    most = jnp.max(top, axis=1, keepdims=True)
    lane = jnp.min(jnp.where(top == most, lanes, BLOCK), axis=1, keepdims=True)
    here = lanes == lane

    def along(x):
        return jnp.sum(jnp.where(slots, x, 0.0), axis=0, keepdims=True)

    picked = [jnp.sum(jnp.where(here, stat_v[n], 0.0), axis=1, keepdims=True) for n in range(1, 5)]
    col_at = along((blocks % 8 * BLOCK + lane).astype(jnp.float32))
    row_at = along((blocks // 8 * BLOCK).astype(jnp.float32) + picked[0])
    ask[...] = jnp.concatenate(
        [jnp.broadcast_to(row_at, (8, BLOCK)), jnp.broadcast_to(col_at, (8, BLOCK))], axis=0
    )

    @pl.loop(1, ND)
    def _(k):
        ask_copy(lax.rem(dp + k, ND), dp).start()

    asked[dp] = ask[...]
    old = [along(x) for x in picked[1:]]

    @pl.loop(1, ND)
    def _(k):
        source = lax.rem(dp + k, ND)
        ask_copy(source, source).wait_recv()

    for half in range(2):
        total = asked[8 * half]
        for n in range(1, 8):
            total = total + asked[8 * half + n]
        rows = total[0:1, :].astype(jnp.int32)
        cols = total[8:9, :].astype(jnp.int32)
        place_v[half] = (
            lax.broadcasted_iota(jnp.int32, (OWN, BLOCK), 0) == rows
        ).astype(jnp.float32).astype(jnp.bfloat16)
        sel_v[half] = jnp.dot(
            g_v[...],
            (lax.broadcasted_iota(jnp.int32, (g_v.shape[1], BLOCK), 0) == cols)
            .astype(jnp.float32)
            .astype(jnp.bfloat16),
            preferred_element_type=jnp.float32,
        )
    answer_v[...] = jnp.zeros_like(answer_v)
    groups = lax.broadcasted_iota(jnp.int32, (8, BLOCK), 1) // NE

    @pl.loop(0, ND)
    def _(o):
        half = o // 8
        chosen = jnp.dot(a_v[o], place_v[half], preferred_element_type=jnp.float32)
        dots = jnp.sum(chosen * sel_v[half], axis=0, keepdims=True)
        answer_v[half] = jnp.where(groups == lax.rem(o, 8), dots, answer_v[half])

    reply[...] = answer_v[...]

    @pl.loop(1, ND)
    def _(k):
        reply_copy(lax.rem(dp + k, ND), dp).start()

    replied[dp] = answer_v[dp // 8]

    @pl.loop(1, ND)
    def _(k):
        source = lax.rem(dp + k, ND)
        reply_copy(source, source).wait_recv()

    exact = replied[0]
    for n in range(1, ND):
        exact = exact + replied[n]
    largest = jnp.abs(adam(*old, exact[0:1, :])[0])
    scale = (largest + 1e-06).astype(jnp.bfloat16).astype(jnp.float32)
    scale = jnp.sum(jnp.where(slots, scale, 0.0), axis=1, keepdims=True)
    for b in range(NE):
        scale_v[b] = jnp.broadcast_to(scale[b : b + 1, :], (8, BLOCK))

    def roll_copy(slot, source):
        return pltpu.make_async_remote_copy(
            src_ref=r_send.at[slot], dst_ref=r_recv.at[source],
            send_sem=r_ss.at[slot], recv_sem=r_rs.at[source],
            device_id=(dp, slot), device_id_type=MESH,
        )

    def held(slot):
        b = jnp.int32(0)
        for n in range(NE):
            b = lax.select(routing[0, 0, n] == slot, jnp.int32(n), b)
        return b

    def pack(ref, b):
        wide = scale_v[b]
        ref[:BLOCK, :] = (wt_v[b] / wide[0:1, :]).astype(jnp.bfloat16)
        ref[BLOCK:, :] = jnp.broadcast_to(wide[0:1, :], (16, BLOCK)).astype(jnp.bfloat16)

    @pl.loop(1, NE)
    def _(k):
        slot = lax.rem(ex + k, NE)
        pack(r_send.at[slot], held(slot))
        roll_copy(slot, ex).start()

    pack(r_recv.at[ex], held(ex))

    @pl.loop(1, NE)
    def _(k):
        source = lax.rem(ex + k, NE)
        roll_copy(source, source).wait_recv()

    row = jnp.zeros((16, BLOCK), jnp.float32)
    for e in range(NE):
        block = r_recv[group_of[e]]
        blocks_out[e] = block[:BLOCK, :]
        row = jnp.where(lanes == e, block[BLOCK:, :].astype(jnp.float32), row)
    scales_out[...] = row.astype(jnp.bfloat16)

    @pl.loop(1, NE)
    def _(k):
        slot = lax.rem(ex + k, NE)
        roll_copy(slot, ex).wait_send()
        peer = lax.rem(dp + k, ND)
        ask_copy(peer, dp).wait_send()
        reply_copy(peer, dp).wait_send()

    @pl.loop(0, 2)
    def _(way):
        for n in range(2):
            s1_copy(way, 0, 2 * way + n).wait_send()
        s2_copy(way, 0, way).wait_send()
        x1_copy(way).wait_send()

        @pl.loop(1, 4)
        def _(s):
            for u in range(4):
                s1_copy(way, s, u).wait_send()
            for c in range(2):
                s2_copy(way, s, c).wait_send()

    @pl.loop(0, 2 * NZ)
    def _(j):
        x2_copy(j).wait_send()

    for c in range(4):
        result(c).wait()


def per_device(acts, out_grads, master, moment_one, moment_two, routing, group_of):
    f32, i16, bf16 = jnp.float32, jnp.int16, jnp.bfloat16
    own, width = master.shape[1], master.shape[2]
    tokens = acts.shape[1]
    dma = pltpu.SemaphoreType.DMA
    hbm = pl.BlockSpec(memory_space=pl.ANY)
    smem = pl.BlockSpec(memory_space=pltpu.SMEM)
    vmem = pl.BlockSpec(memory_space=pltpu.VMEM)
    shape = jax.ShapeDtypeStruct
    grad, blocks, scales = pl.pallas_call(
        kernel,
        out_shape=(
            shape((own, width), f32),
            shape((NE, BLOCK, BLOCK), bf16),
            shape((16, BLOCK), bf16),
        ),
        in_specs=[hbm] * 5 + [smem] * 2,
        out_specs=(hbm, vmem, vmem),
        scratch_shapes=[
            pltpu.VMEM((2 * NZ, tokens, OWN), bf16),
            pltpu.VMEM((tokens, width), bf16),
            pltpu.VMEM((own, width), f32),
            pltpu.VMEM((own, width), f32),
            pltpu.VMEM((own, width), f32),
            pltpu.VMEM((NE, BLOCK, BLOCK), f32),
            pltpu.VMEM((own, width), f32),
            pltpu.VMEM((2, 4, 4, MSG, BLOCK), i16),
            pltpu.VMEM((2, 4, 4, MSG, BLOCK), i16),
            pltpu.VMEM((2, 4, 2, MSG, BLOCK), i16),
            pltpu.VMEM((2, 4, 2, MSG, BLOCK), i16),
            pltpu.VMEM((2 * NZ, MSG, BLOCK), i16),
            pltpu.VMEM((2 * NZ, MSG, BLOCK), i16),
            pltpu.VMEM((2, MSG, BLOCK), i16),
            pltpu.VMEM((2, MSG, BLOCK), i16),
            pltpu.VMEM((16, BLOCK), f32),
            pltpu.VMEM((ND, 16, BLOCK), f32),
            pltpu.VMEM((2, 8, BLOCK), f32),
            pltpu.VMEM((ND, 8, BLOCK), f32),
            pltpu.VMEM((5, NE, BLOCK), f32),
            pltpu.VMEM((2, tokens, BLOCK), f32),
            pltpu.VMEM((2, own, BLOCK), bf16),
            pltpu.VMEM((2, 8, BLOCK), f32),
            pltpu.VMEM((NE, 8, BLOCK), f32),
            pltpu.VMEM((NE, BLOCK + 16, BLOCK), bf16),
            pltpu.VMEM((NE, BLOCK + 16, BLOCK), bf16),
            dma((2 * NZ,)),
            dma((4,)),
            dma((4,)),
            dma((2, 4, 4)),
            dma((2, 4, 4)),
            dma((2, 4, 2)),
            dma((2, 4, 2)),
            dma((2 * NZ,)),
            dma((2 * NZ,)),
            dma((2,)),
            dma((2,)),
            dma((ND,)),
            dma((ND,)),
            dma((ND,)),
            dma((ND,)),
            dma((NE,)),
            dma((NE,)),
        ],
        name="update",
        cost_estimate=pl.CostEstimate(
            flops=2 * tokens * acts.shape[2] * width, bytes_accessed=12 * 2**20, transcendentals=0
        ),
        compiler_params=pltpu.CompilerParams(
            collective_id=0, has_side_effects=True, vmem_limit_bytes=56 * 2**20
        ),
    )(acts, out_grads, master, moment_one, moment_two, routing, group_of)
    weight, first, second = adam(master[0], moment_one[0], moment_two[0], grad)
    return (
        weight[None],
        first[None],
        second[None],
        blocks.reshape(1, 1, NE, 1, BLOCK, BLOCK),
        scales[0, :NE].reshape(1, 1, NE, 1),
    )


def solution(mesh):
    in_specs = (P("expert", "dp", None),) * 6 + (P(),)
    out_specs = (
        P("expert", "dp", None),
        P("expert", "dp", None),
        P("expert", "dp", None),
        P("expert", "dp", None, None, None, None),
        P("expert", "dp", None, None),
    )
    return jax.shard_map(
        per_device, mesh=mesh, in_specs=in_specs, out_specs=out_specs, check_vma=False
    )
```

```python
import math

import jax
import jax.numpy as jnp
from jax import lax
from jax.experimental import pallas as pl
from jax.experimental.pallas import tpu as pltpu
from jax.sharding import PartitionSpec as P

MESH = pl.DeviceIdType.MESH
BLOCK = 128
NZ = 8
ND = 16
NE = 16
OWN = 256
UC = 256
MSG = 2 * OWN + 16
LEVELS = 32766.0
FINE = 8.0
LN2 = math.log(2.0)

beta_one = 0.9
beta_two = 0.95
learn_rate = 0.01
decay_rate = 0.1
adam_eps = 1e-08
corr_one = 1.0 - 0.9**10
corr_two = 1.0 - 0.95**10

ORDER = (
    0, 18, 128, 1, 19, 129, 20, 130, 141, 6, 21, 134, 7, 86,
    68, 69, 87, 132, 133, 89, 192, 209, 74, 88, 73, 131, 138, 139,
    75, 135, 212, 91, 72, 277, 90, 260, 78, 136, 79, 137, 77, 93,
    197, 142, 143, 95, 92, 140, 264, 76, 280, 94, 321, 265, 281, 284,
    268, 320, 269, 285, 384, 448, 385, 449,
)
HEAD = 6


def pick(k, values):
    if len(set(values)) == 1:
        return jnp.int32(values[0])
    half = len(values) // 2
    return lax.select(k < half, pick(k, values[:half]), pick(k - half, values[half:]))


def adam(weight, one, two, grad):
    first = beta_one * one + (1.0 - beta_one) * grad
    second = beta_two * two + (1.0 - beta_two) * grad * grad
    update = (first * (1.0 / corr_one)) / (
        jnp.sqrt(second * (1.0 / corr_two)) + adam_eps
    ) + decay_rate * weight
    return weight - learn_rate * update, first, second


def encode(ref, halves):
    steps = []
    for h, v in enumerate(halves):
        top = jnp.max(jnp.abs(v), axis=0, keepdims=True)
        step = jnp.ceil(jnp.log(jnp.maximum(top, 2.0**-100)) * (FINE / LN2))
        inv = jnp.exp(step * (-LN2 / FINE)) * LEVELS
        ref[h * OWN : (h + 1) * OWN, :] = jnp.round(v * inv).astype(jnp.int32).astype(jnp.int16)
        steps.append(jnp.broadcast_to(step, (8, BLOCK)))
    ref[2 * OWN :, :] = jnp.concatenate(steps, axis=0).astype(jnp.int32).astype(jnp.int16)


def decode(ref):
    steps = ref[2 * OWN :, :].astype(jnp.int32).astype(jnp.float32)
    scales = jnp.exp(steps * (LN2 / FINE)) * (1.0 / LEVELS)
    return [
        ref[h * OWN : (h + 1) * OWN, :].astype(jnp.int32).astype(jnp.float32)
        * scales[8 * h : 8 * h + 1, :]
        for h in range(2)
    ]


def kernel(
    acts, grads, master, moment_one, moment_two, routing, group_of,
    grad_out, blocks_out, scales_out,
    a_v, g_v, w_v, m_v, v_v, wt_v, sum_v,
    s1_send, s1_recv, s2_send, s2_recv, x2_send, x2_recv, x1_send, x1_recv, ask, asked, reply, replied,
    stat_v, sel_v, place_v, answer_v, scale_v, r_send, r_recv, c_send, c_recv,
    a_sem, in_sem, out_sem,
    s1_ss, s1_rs, s2_ss, s2_rs, x2_ss, x2_rs, x1_ss, x1_rs, ask_ss, ask_rs, rep_ss, rep_rs, r_ss, r_rs, c_ss, c_rs,
):
    dp = lax.axis_index("dp")
    ex = lax.axis_index("expert")
    z, xh = dp // 2, dp % 2

    def zdev(way):
        return (lax.rem(z + 1 + 6 * way, NZ) * 2 + xh, ex)

    partner = (z * 2 + 1 - xh, ex)
    mine = z * 2 + xh

    def load_acts(off, half):
        i = lax.rem(z + off, NZ) * 2 + half
        return pltpu.make_async_copy(
            acts.at[0, :, pl.ds(pl.multiple_of(i * OWN, OWN), OWN)], a_v.at[i], a_sem.at[i]
        )

    grads_copy = pltpu.make_async_copy(grads.at[0], g_v, in_sem.at[0])
    load_acts(4, 0).start()
    grads_copy.start()
    load_acts(4, 1).start()
    order = (3, 5, 2, 6, 1, 7, 0)
    for off in order:
        for half in range(2):
            load_acts(off, half).start()
    state = [
        pltpu.make_async_copy(src.at[0], dst, in_sem.at[1 + i])
        for i, (src, dst) in enumerate(((master, w_v), (moment_one, m_v), (moment_two, v_v)))
    ]
    for c in state:
        c.start()

    barrier = pltpu.get_barrier_semaphore()

    @pl.loop(1, NE)
    def _(k):
        pl.semaphore_signal(barrier, inc=1, device_id=(lax.rem(dp + k, ND), ex), device_id_type=MESH)
        pl.semaphore_signal(barrier, inc=1, device_id=(dp, lax.rem(ex + k, NE)), device_id_type=MESH)

    pl.semaphore_wait(barrier, ND - 1 + NE - 1)

    def partial(i, c):
        p = lax.dot_general(
            a_v[i],
            g_v[:, pl.ds(pl.multiple_of(c * UC, UC), UC)],
            (((0,), (0,)), ((), ())),
            preferred_element_type=jnp.float32,
        )
        return [p[:, :BLOCK], p[:, BLOCK:]]

    def add(a, b):
        return [u + v for u, v in zip(a, b)]

    def s1_copy(way, s, u):
        return pltpu.make_async_remote_copy(
            src_ref=s1_send.at[way, s, u], dst_ref=s1_recv.at[way, s, u],
            send_sem=s1_ss.at[way, s, u], recv_sem=s1_rs.at[way, s, u],
            device_id=zdev(way), device_id_type=MESH,
        )

    def s2_copy(way, s, c):
        return pltpu.make_async_remote_copy(
            src_ref=s2_send.at[way, s, c], dst_ref=s2_recv.at[way, s, c],
            send_sem=s2_ss.at[way, s, c], recv_sem=s2_rs.at[way, s, c],
            device_id=zdev(way), device_id_type=MESH,
        )

    def x2_copy(j):
        return pltpu.make_async_remote_copy(
            src_ref=x2_send.at[j], dst_ref=x2_recv.at[j],
            send_sem=x2_ss.at[j], recv_sem=x2_rs.at[j],
            device_id=partner, device_id_type=MESH,
        )

    def x1_copy(c):
        return pltpu.make_async_remote_copy(
            src_ref=x1_send.at[c], dst_ref=x1_recv.at[c],
            send_sem=x1_ss.at[c], recv_sem=x1_rs.at[c],
            device_id=partner, device_id_type=MESH,
        )

    def target(way, s):
        return lax.rem(z + 4 + (1 - 2 * way) * (-s) + NZ, NZ)

    def s1_task(way, s, u, arrived):
        v = partial(target(way, s) * 2 + u // 2, u % 2)
        if arrived:
            s1_copy(way, s - 1, u).wait_recv()
            v = add(v, decode(s1_recv.at[way, s - 1, u]))
        encode(s1_send.at[way, s, u], v)
        s1_copy(way, s, u).start()

    def x2_task(j):
        o = j // 2
        off = lax.select(o % 2 == 1, 4 - (o + 1) // 2, 4 + o // 2)
        encode(x2_send.at[j], partial(lax.rem(z + off, NZ) * 2 + 1 - xh, 2 + j % 2))
        x2_copy(j).start()

    def s2_task(way, s, c, arrived):
        v = partial(target(way, s) * 2 + xh, 2 + c)
        j = lax.select(s == 0, c, (2 * s - 1 + way) * 2 + c)
        x2_copy(j).wait_recv()
        v = add(v, decode(x2_recv.at[j]))
        if arrived:
            s2_copy(way, s - 1, c).wait_recv()
            v = add(v, decode(s2_recv.at[way, s - 1, c]))
        encode(s2_send.at[way, s, c], v)
        s2_copy(way, s, c).start()

    def s1_sum(half, c):
        u = 2 * half + c
        v = partial(z * 2 + half, c)
        for way in range(2):
            s1_copy(way, 3, u).wait_recv()
            v = add(v, decode(s1_recv.at[way, 3, u]))
        return v

    def result(c):
        cols = pl.ds(pl.multiple_of(c * UC, UC), UC)
        return pltpu.make_async_copy(sum_v.at[:, cols], grad_out.at[:, cols], out_sem.at[c])

    row_ids = lax.broadcasted_iota(jnp.int32, (BLOCK, BLOCK), 0)

    def finish(c, halves):
        for h, grad in enumerate(halves):
            cols = pl.ds(pl.multiple_of(c * UC + h * BLOCK, BLOCK), BLOCK)
            sum_v[:, cols] = grad
            weight = adam(w_v[:, cols], m_v[:, cols], v_v[:, cols], grad)[0]
            for r in range(2):
                b = r * 8 + 2 * c + h
                rows = slice(r * BLOCK, (r + 1) * BLOCK)
                tile = weight[rows, :]
                wt_v[b] = tile
                size = jnp.abs(tile)
                top = jnp.max(size, axis=0, keepdims=True)
                at = jnp.min(jnp.where(size == top, row_ids, BLOCK), axis=0, keepdims=True)
                one_row = row_ids == at
                stat_v[0, pl.ds(b, 1), :] = top
                stat_v[1, pl.ds(b, 1), :] = at.astype(jnp.float32)
                for n, src in enumerate((w_v, m_v, v_v)):
                    stat_v[2 + n, pl.ds(b, 1), :] = jnp.sum(
                        jnp.where(one_row, src[rows, cols], 0.0), axis=0, keepdims=True
                    )
        result(c).start()

    def x1_task(c):
        encode(x1_send.at[c], s1_sum(1 - xh, c))
        x1_copy(c).start()

    def finish_s1(c):
        v = s1_sum(xh, c)
        x1_copy(c).wait_recv()
        finish(c, add(v, decode(x1_recv.at[c])))

    def finish_s2(c):
        v = partial(mine, 2 + c)
        x2_copy(14 + c).wait_recv()
        v = add(v, decode(x2_recv.at[14 + c]))
        for way in range(2):
            s2_copy(way, 3, c).wait_recv()
            v = add(v, decode(s2_recv.at[way, 3, c]))
        finish(2 + c, v)

    load_acts(4, 0).wait()
    grads_copy.wait()
    load_acts(4, 1).wait()

    @pl.loop(0, len(ORDER))
    def _(k):
        @pl.when(k == HEAD)
        def _():
            for off in order:
                for half in range(2):
                    load_acts(off, half).wait()
            for c in state:
                c.wait()

        code = pick(k, ORDER)
        kind = code // 64
        way, s, u = code // 16 % 4, code // 4 % 4, code % 4
        for n, task in enumerate(
            (
                lambda: s1_task(way, s, u, False),
                lambda: s1_task(way, s, u, True),
                lambda: x2_task(code % 64),
                lambda: s2_task(way, s, u, False),
                lambda: s2_task(way, s, u, True),
                lambda: x1_task(u),
                lambda: finish_s1(u),
                lambda: finish_s2(u),
            )
        ):
            pl.when(kind == n)(task)

    def ask_copy(peer, source):
        return pltpu.make_async_remote_copy(
            src_ref=ask, dst_ref=asked.at[source],
            send_sem=ask_ss.at[peer], recv_sem=ask_rs.at[source],
            device_id=(peer, ex), device_id_type=MESH,
        )

    def reply_copy(peer, source):
        return pltpu.make_async_remote_copy(
            src_ref=reply.at[peer // 8], dst_ref=replied.at[source],
            send_sem=rep_ss.at[peer], recv_sem=rep_rs.at[source],
            device_id=(peer, ex), device_id_type=MESH,
        )

    lanes = lax.broadcasted_iota(jnp.int32, (NE, BLOCK), 1)
    blocks = lax.broadcasted_iota(jnp.int32, (NE, BLOCK), 0)
    slots = lanes == lax.rem(dp, 8) * NE + blocks
    top = stat_v[0]
    most = jnp.max(top, axis=1, keepdims=True)
    lane = jnp.min(jnp.where(top == most, lanes, BLOCK), axis=1, keepdims=True)
    here = lanes == lane

    def along(x):
        return jnp.sum(jnp.where(slots, x, 0.0), axis=0, keepdims=True)

    picked = [jnp.sum(jnp.where(here, stat_v[n], 0.0), axis=1, keepdims=True) for n in range(1, 5)]
    col_at = along((blocks % 8 * BLOCK + lane).astype(jnp.float32))
    row_at = along((blocks // 8 * BLOCK).astype(jnp.float32) + picked[0])
    ask[...] = jnp.concatenate(
        [jnp.broadcast_to(row_at, (8, BLOCK)), jnp.broadcast_to(col_at, (8, BLOCK))], axis=0
    )

    @pl.loop(1, ND)
    def _(k):
        ask_copy(lax.rem(dp + k, ND), dp).start()

    asked[dp] = ask[...]

    def roll_copy(slot, source):
        return pltpu.make_async_remote_copy(
            src_ref=r_send.at[slot], dst_ref=r_recv.at[source],
            send_sem=r_ss.at[slot], recv_sem=r_rs.at[source],
            device_id=(dp, slot), device_id_type=MESH,
        )

    def scale_copy(slot, source):
        return pltpu.make_async_remote_copy(
            src_ref=c_send.at[slot], dst_ref=c_recv.at[source],
            send_sem=c_ss.at[slot], recv_sem=c_rs.at[source],
            device_id=(dp, slot), device_id_type=MESH,
        )

    def held(slot):
        b = jnp.int32(0)
        for n in range(NE):
            b = lax.select(routing[0, 0, n] == slot, jnp.int32(n), b)
        return b

    @pl.loop(1, NE)
    def _(k):
        slot = lax.rem(ex + k, NE)
        r_send[slot] = wt_v[held(slot)]
        roll_copy(slot, ex).start()

    r_recv[ex] = wt_v[held(ex)]
    old = [along(x) for x in picked[1:]]

    @pl.loop(1, ND)
    def _(k):
        source = lax.rem(dp + k, ND)
        ask_copy(source, source).wait_recv()

    for half in range(2):
        total = asked[8 * half]
        for n in range(1, 8):
            total = total + asked[8 * half + n]
        rows = total[0:1, :].astype(jnp.int32)
        cols = total[8:9, :].astype(jnp.int32)
        place_v[half] = (
            lax.broadcasted_iota(jnp.int32, (OWN, BLOCK), 0) == rows
        ).astype(jnp.float32).astype(jnp.bfloat16)
        sel_v[half] = jnp.dot(
            g_v[...],
            (lax.broadcasted_iota(jnp.int32, (g_v.shape[1], BLOCK), 0) == cols)
            .astype(jnp.float32)
            .astype(jnp.bfloat16),
            preferred_element_type=jnp.float32,
        )
    answer_v[...] = jnp.zeros_like(answer_v)
    groups = lax.broadcasted_iota(jnp.int32, (8, BLOCK), 1) // NE

    @pl.loop(0, ND)
    def _(o):
        half = o // 8
        chosen = jnp.dot(a_v[o], place_v[half], preferred_element_type=jnp.float32)
        dots = jnp.sum(chosen * sel_v[half], axis=0, keepdims=True)
        answer_v[half] = jnp.where(groups == lax.rem(o, 8), dots, answer_v[half])

    reply[...] = answer_v[...]

    @pl.loop(1, ND)
    def _(k):
        reply_copy(lax.rem(dp + k, ND), dp).start()

    replied[dp] = answer_v[dp // 8]

    @pl.loop(1, ND)
    def _(k):
        source = lax.rem(dp + k, ND)
        reply_copy(source, source).wait_recv()

    exact = replied[0]
    for n in range(1, ND):
        exact = exact + replied[n]
    largest = jnp.abs(adam(*old, exact[0:1, :])[0])
    scale = (largest + 1e-06).astype(jnp.bfloat16).astype(jnp.float32)
    scale = jnp.sum(jnp.where(slots, scale, 0.0), axis=1, keepdims=True)
    for b in range(NE):
        scale_v[b] = jnp.broadcast_to(scale[b : b + 1, :], (8, BLOCK))

    @pl.loop(1, NE)
    def _(k):
        slot = lax.rem(ex + k, NE)
        c_send[slot] = scale_v[held(slot)]
        scale_copy(slot, ex).start()

    c_recv[ex] = scale_v[held(ex)]

    @pl.loop(1, NE)
    def _(k):
        source = lax.rem(ex + k, NE)
        roll_copy(source, source).wait_recv()

    @pl.loop(1, NE)
    def _(k):
        source = lax.rem(ex + k, NE)
        scale_copy(source, source).wait_recv()

    row = jnp.zeros((16, BLOCK), jnp.float32)
    for e in range(NE):
        g = group_of[e]
        wide = c_recv[g]
        blocks_out[e] = (r_recv[g] / wide[0:1, :]).astype(jnp.bfloat16)
        row = jnp.where(lanes == e, wide[0:1, :], row)
    scales_out[...] = row.astype(jnp.bfloat16)

    @pl.loop(1, NE)
    def _(k):
        slot = lax.rem(ex + k, NE)
        roll_copy(slot, ex).wait_send()
        scale_copy(slot, ex).wait_send()
        peer = lax.rem(dp + k, ND)
        ask_copy(peer, dp).wait_send()
        reply_copy(peer, dp).wait_send()

    @pl.loop(0, 2)
    def _(way):
        for n in range(2):
            s1_copy(way, 0, 2 * way + n).wait_send()
        s2_copy(way, 0, way).wait_send()
        x1_copy(way).wait_send()

        @pl.loop(1, 4)
        def _(s):
            for u in range(4):
                s1_copy(way, s, u).wait_send()
            for c in range(2):
                s2_copy(way, s, c).wait_send()

    @pl.loop(0, 2 * NZ)
    def _(j):
        x2_copy(j).wait_send()

    for c in range(4):
        result(c).wait()


def per_device(acts, out_grads, master, moment_one, moment_two, routing, group_of):
    f32, i16, bf16 = jnp.float32, jnp.int16, jnp.bfloat16
    own, width = master.shape[1], master.shape[2]
    tokens = acts.shape[1]
    dma = pltpu.SemaphoreType.DMA
    hbm = pl.BlockSpec(memory_space=pl.ANY)
    smem = pl.BlockSpec(memory_space=pltpu.SMEM)
    vmem = pl.BlockSpec(memory_space=pltpu.VMEM)
    shape = jax.ShapeDtypeStruct
    grad, blocks, scales = pl.pallas_call(
        kernel,
        out_shape=(
            shape((own, width), f32),
            shape((NE, BLOCK, BLOCK), bf16),
            shape((16, BLOCK), bf16),
        ),
        in_specs=[hbm] * 5 + [smem] * 2,
        out_specs=(hbm, vmem, vmem),
        scratch_shapes=[
            pltpu.VMEM((2 * NZ, tokens, OWN), bf16),
            pltpu.VMEM((tokens, width), bf16),
            pltpu.VMEM((own, width), f32),
            pltpu.VMEM((own, width), f32),
            pltpu.VMEM((own, width), f32),
            pltpu.VMEM((NE, BLOCK, BLOCK), f32),
            pltpu.VMEM((own, width), f32),
            pltpu.VMEM((2, 4, 4, MSG, BLOCK), i16),
            pltpu.VMEM((2, 4, 4, MSG, BLOCK), i16),
            pltpu.VMEM((2, 4, 2, MSG, BLOCK), i16),
            pltpu.VMEM((2, 4, 2, MSG, BLOCK), i16),
            pltpu.VMEM((2 * NZ, MSG, BLOCK), i16),
            pltpu.VMEM((2 * NZ, MSG, BLOCK), i16),
            pltpu.VMEM((2, MSG, BLOCK), i16),
            pltpu.VMEM((2, MSG, BLOCK), i16),
            pltpu.VMEM((16, BLOCK), f32),
            pltpu.VMEM((ND, 16, BLOCK), f32),
            pltpu.VMEM((2, 8, BLOCK), f32),
            pltpu.VMEM((ND, 8, BLOCK), f32),
            pltpu.VMEM((5, NE, BLOCK), f32),
            pltpu.VMEM((2, tokens, BLOCK), f32),
            pltpu.VMEM((2, own, BLOCK), bf16),
            pltpu.VMEM((2, 8, BLOCK), f32),
            pltpu.VMEM((NE, 8, BLOCK), f32),
            pltpu.VMEM((NE, BLOCK, BLOCK), f32),
            pltpu.VMEM((NE, BLOCK, BLOCK), f32),
            pltpu.VMEM((NE, 8, BLOCK), f32),
            pltpu.VMEM((NE, 8, BLOCK), f32),
            dma((2 * NZ,)),
            dma((4,)),
            dma((4,)),
            dma((2, 4, 4)),
            dma((2, 4, 4)),
            dma((2, 4, 2)),
            dma((2, 4, 2)),
            dma((2 * NZ,)),
            dma((2 * NZ,)),
            dma((2,)),
            dma((2,)),
            dma((ND,)),
            dma((ND,)),
            dma((ND,)),
            dma((ND,)),
            dma((NE,)),
            dma((NE,)),
            dma((NE,)),
            dma((NE,)),
        ],
        name="update",
        cost_estimate=pl.CostEstimate(
            flops=2 * tokens * acts.shape[2] * width, bytes_accessed=12 * 2**20, transcendentals=0
        ),
        compiler_params=pltpu.CompilerParams(
            collective_id=0, has_side_effects=True, vmem_limit_bytes=56 * 2**20
        ),
    )(acts, out_grads, master, moment_one, moment_two, routing, group_of)
    weight, first, second = adam(master[0], moment_one[0], moment_two[0], grad)
    return (
        weight[None],
        first[None],
        second[None],
        blocks.reshape(1, 1, NE, 1, BLOCK, BLOCK),
        scales[0, :NE].reshape(1, 1, NE, 1),
    )


def solution(mesh):
    in_specs = (P("expert", "dp", None),) * 6 + (P(),)
    out_specs = (
        P("expert", "dp", None),
        P("expert", "dp", None),
        P("expert", "dp", None),
        P("expert", "dp", None, None, None, None),
        P("expert", "dp", None, None),
    )
    return jax.shard_map(
        per_device, mesh=mesh, in_specs=in_specs, out_specs=out_specs, check_vma=False
    )
```

```python
import math

import jax
import jax.numpy as jnp
from jax import lax
from jax.experimental import pallas as pl
from jax.experimental.pallas import tpu as pltpu
from jax.sharding import PartitionSpec as P

MESH = pl.DeviceIdType.MESH
BLOCK = 128
NZ = 8
ND = 16
NE = 16
OWN = 256
UC = 256
MSG = 2 * OWN + 16
LEVELS = 32766.0
FINE = 8.0
LN2 = math.log(2.0)

beta_one = 0.9
beta_two = 0.95
learn_rate = 0.01
decay_rate = 0.1
adam_eps = 1e-08
corr_one = 1.0 - 0.9**10
corr_two = 1.0 - 0.95**10

ORDER = (
    0, 18, 128, 1, 19, 129, 20, 130, 141, 6, 21, 134, 7, 86,
    68, 69, 87, 132, 133, 89, 192, 209, 74, 88, 73, 131, 138, 139,
    75, 135, 212, 91, 72, 277, 90, 260, 78, 136, 79, 137, 77, 93,
    197, 142, 143, 95, 92, 140, 264, 76, 280, 94, 321, 265, 281, 284,
    268, 320, 269, 285, 384, 448, 385, 449,
)
HEAD = 6


def pick(k, values):
    if len(set(values)) == 1:
        return jnp.int32(values[0])
    half = len(values) // 2
    return lax.select(k < half, pick(k, values[:half]), pick(k - half, values[half:]))


def moments(one, two, grad):
    first = beta_one * one + (1.0 - beta_one) * grad
    second = beta_two * two + (1.0 - beta_two) * grad * grad
    return first, second


def adam(weight, one, two, grad):
    first, second = moments(one, two, grad)
    update = (first * (1.0 / corr_one)) / (
        jnp.sqrt(second * (1.0 / corr_two)) + adam_eps
    ) + decay_rate * weight
    return learn_rate * update


def encode(ref, halves):
    steps = []
    for h, v in enumerate(halves):
        top = jnp.max(jnp.abs(v), axis=0, keepdims=True)
        step = jnp.ceil(jnp.log(jnp.maximum(top, 2.0**-100)) * (FINE / LN2))
        inv = jnp.exp(step * (-LN2 / FINE)) * LEVELS
        ref[h * OWN : (h + 1) * OWN, :] = jnp.round(v * inv).astype(jnp.int32).astype(jnp.int16)
        steps.append(jnp.broadcast_to(step, (8, BLOCK)))
    ref[2 * OWN :, :] = jnp.concatenate(steps, axis=0).astype(jnp.int32).astype(jnp.int16)


def decode(ref):
    steps = ref[2 * OWN :, :].astype(jnp.int32).astype(jnp.float32)
    scales = jnp.exp(steps * (LN2 / FINE)) * (1.0 / LEVELS)
    return [
        ref[h * OWN : (h + 1) * OWN, :].astype(jnp.int32).astype(jnp.float32)
        * scales[8 * h : 8 * h + 1, :]
        for h in range(2)
    ]


def kernel(
    acts, grads, master, moment_one, moment_two, routing, group_of,
    grad_out, step_out, blocks_out, scales_out,
    a_v, g_v, w_v, m_v, v_v, wt_v, sum_v, step_v,
    s1_send, s1_recv, s2_send, s2_recv, x2_send, x2_recv, x1_send, x1_recv, ask, asked, reply, replied,
    stat_v, sel_v, place_v, scale_v, r_send, r_recv, c_send, c_recv,
    a_sem, in_sem, out_sem,
    s1_ss, s1_rs, s2_ss, s2_rs, x2_ss, x2_rs, x1_ss, x1_rs, ask_ss, ask_rs, rep_ss, rep_rs, r_ss, r_rs, c_ss, c_rs,
):
    dp = lax.axis_index("dp")
    ex = lax.axis_index("expert")
    z, xh = dp // 2, dp % 2

    def zdev(way):
        return (lax.rem(z + 1 + 6 * way, NZ) * 2 + xh, ex)

    partner = (z * 2 + 1 - xh, ex)

    def owner(dz, other):
        return lax.rem(z + dz, NZ) * 2 + lax.rem(xh + other, 2)

    mine = z * 2 + xh

    def load_acts(off, half):
        i = lax.rem(z + off, NZ) * 2 + half
        return pltpu.make_async_copy(
            acts.at[0, :, pl.ds(pl.multiple_of(i * OWN, OWN), OWN)], a_v.at[i], a_sem.at[i]
        )

    grads_copy = pltpu.make_async_copy(grads.at[0], g_v, in_sem.at[0])
    load_acts(4, 0).start()
    grads_copy.start()
    load_acts(4, 1).start()
    order = (3, 5, 2, 6, 1, 7, 0)
    for off in order:
        for half in range(2):
            load_acts(off, half).start()
    state = [
        pltpu.make_async_copy(src.at[0], dst, in_sem.at[1 + i])
        for i, (src, dst) in enumerate(((master, w_v), (moment_one, m_v), (moment_two, v_v)))
    ]
    for c in state:
        c.start()

    barrier = pltpu.get_barrier_semaphore()

    @pl.loop(1, NE)
    def _(k):
        pl.semaphore_signal(barrier, inc=1, device_id=(lax.rem(dp + k, ND), ex), device_id_type=MESH)
        pl.semaphore_signal(barrier, inc=1, device_id=(dp, lax.rem(ex + k, NE)), device_id_type=MESH)

    pl.semaphore_wait(barrier, ND - 1 + NE - 1)

    def partial(i, c):
        p = lax.dot_general(
            a_v[i],
            g_v[:, pl.ds(pl.multiple_of(c * UC, UC), UC)],
            (((0,), (0,)), ((), ())),
            preferred_element_type=jnp.float32,
        )
        return [p[:, :BLOCK], p[:, BLOCK:]]

    def add(a, b):
        return [u + v for u, v in zip(a, b)]

    def s1_copy(way, s, u):
        return pltpu.make_async_remote_copy(
            src_ref=s1_send.at[way, s, u], dst_ref=s1_recv.at[way, s, u],
            send_sem=s1_ss.at[way, s, u], recv_sem=s1_rs.at[way, s, u],
            device_id=zdev(way), device_id_type=MESH,
        )

    def s2_copy(way, s, c):
        return pltpu.make_async_remote_copy(
            src_ref=s2_send.at[way, s, c], dst_ref=s2_recv.at[way, s, c],
            send_sem=s2_ss.at[way, s, c], recv_sem=s2_rs.at[way, s, c],
            device_id=zdev(way), device_id_type=MESH,
        )

    def x2_copy(j):
        return pltpu.make_async_remote_copy(
            src_ref=x2_send.at[j], dst_ref=x2_recv.at[j],
            send_sem=x2_ss.at[j], recv_sem=x2_rs.at[j],
            device_id=partner, device_id_type=MESH,
        )

    def x1_copy(c):
        return pltpu.make_async_remote_copy(
            src_ref=x1_send.at[c], dst_ref=x1_recv.at[c],
            send_sem=x1_ss.at[c], recv_sem=x1_rs.at[c],
            device_id=partner, device_id_type=MESH,
        )

    def target(way, s):
        return lax.rem(z + 4 + (1 - 2 * way) * (-s) + NZ, NZ)

    def s1_task(way, s, u, arrived):
        v = partial(target(way, s) * 2 + u // 2, u % 2)
        if arrived:
            s1_copy(way, s - 1, u).wait_recv()
            v = add(v, decode(s1_recv.at[way, s - 1, u]))
        encode(s1_send.at[way, s, u], v)
        s1_copy(way, s, u).start()

    def x2_task(j):
        o = j // 2
        off = lax.select(o % 2 == 1, 4 - (o + 1) // 2, 4 + o // 2)
        encode(x2_send.at[j], partial(lax.rem(z + off, NZ) * 2 + 1 - xh, 2 + j % 2))
        x2_copy(j).start()

    def s2_task(way, s, c, arrived):
        v = partial(target(way, s) * 2 + xh, 2 + c)
        j = lax.select(s == 0, c, (2 * s - 1 + way) * 2 + c)
        x2_copy(j).wait_recv()
        v = add(v, decode(x2_recv.at[j]))
        if arrived:
            s2_copy(way, s - 1, c).wait_recv()
            v = add(v, decode(s2_recv.at[way, s - 1, c]))
        encode(s2_send.at[way, s, c], v)
        s2_copy(way, s, c).start()

    def s1_sum(half, c):
        u = 2 * half + c
        v = partial(z * 2 + half, c)
        for way in range(2):
            s1_copy(way, 3, u).wait_recv()
            v = add(v, decode(s1_recv.at[way, 3, u]))
        return v

    def result(c):
        cols = pl.ds(pl.multiple_of(c * UC, UC), UC)
        return [
            pltpu.make_async_copy(src.at[:, cols], dst.at[:, cols], out_sem.at[n, c])
            for n, (src, dst) in enumerate(((sum_v, grad_out), (step_v, step_out)))
        ]

    row_ids = lax.broadcasted_iota(jnp.int32, (BLOCK, BLOCK), 0)

    def finish(c, halves):
        for h, grad in enumerate(halves):
            cols = pl.ds(pl.multiple_of(c * UC + h * BLOCK, BLOCK), BLOCK)
            sum_v[:, cols] = grad
            step = adam(w_v[:, cols], m_v[:, cols], v_v[:, cols], grad)
            step_v[:, cols] = step
            weight = w_v[:, cols] - step
            for r in range(2):
                b = r * 8 + 2 * c + h
                rows = slice(r * BLOCK, (r + 1) * BLOCK)
                tile = weight[rows, :]
                wt_v[b] = tile
                size = jnp.abs(tile)
                top = jnp.max(size, axis=0, keepdims=True)
                at = jnp.min(jnp.where(size == top, row_ids, BLOCK), axis=0, keepdims=True)
                one_row = row_ids == at
                stat_v[0, pl.ds(b, 1), :] = top
                stat_v[1, pl.ds(b, 1), :] = at.astype(jnp.float32)
                for n, src in enumerate((w_v, m_v, v_v)):
                    stat_v[2 + n, pl.ds(b, 1), :] = jnp.sum(
                        jnp.where(one_row, src[rows, cols], 0.0), axis=0, keepdims=True
                    )
        for copy in result(c):
            copy.start()

    def x1_task(c):
        encode(x1_send.at[c], s1_sum(1 - xh, c))
        x1_copy(c).start()

    def finish_s1(c):
        v = s1_sum(xh, c)
        x1_copy(c).wait_recv()
        finish(c, add(v, decode(x1_recv.at[c])))

    def finish_s2(c):
        v = partial(mine, 2 + c)
        x2_copy(14 + c).wait_recv()
        v = add(v, decode(x2_recv.at[14 + c]))
        for way in range(2):
            s2_copy(way, 3, c).wait_recv()
            v = add(v, decode(s2_recv.at[way, 3, c]))
        finish(2 + c, v)

    load_acts(4, 0).wait()
    grads_copy.wait()
    load_acts(4, 1).wait()

    @pl.loop(0, len(ORDER))
    def _(k):
        @pl.when(k == HEAD)
        def _():
            for off in order:
                for half in range(2):
                    load_acts(off, half).wait()
            for c in state:
                c.wait()

        code = pick(k, ORDER)
        kind = code // 64
        way, s, u = code // 16 % 4, code // 4 % 4, code % 4
        for n, task in enumerate(
            (
                lambda: s1_task(way, s, u, False),
                lambda: s1_task(way, s, u, True),
                lambda: x2_task(code % 64),
                lambda: s2_task(way, s, u, False),
                lambda: s2_task(way, s, u, True),
                lambda: x1_task(u),
                lambda: finish_s1(u),
                lambda: finish_s2(u),
            )
        ):
            pl.when(kind == n)(task)

    def ask_copy(peer, source):
        return pltpu.make_async_remote_copy(
            src_ref=ask, dst_ref=asked.at[source],
            send_sem=ask_ss.at[peer], recv_sem=ask_rs.at[source],
            device_id=(peer, ex), device_id_type=MESH,
        )

    def reply_copy(peer, source):
        return pltpu.make_async_remote_copy(
            src_ref=reply.at[lax.rem(peer + dp, 2)], dst_ref=replied.at[source],
            send_sem=rep_ss.at[peer], recv_sem=rep_rs.at[source],
            device_id=(peer, ex), device_id_type=MESH,
        )

    lanes = lax.broadcasted_iota(jnp.int32, (NE, BLOCK), 1)
    blocks = lax.broadcasted_iota(jnp.int32, (NE, BLOCK), 0)
    slots = lanes % NE == blocks
    top = stat_v[0]
    most = jnp.max(top, axis=1, keepdims=True)
    lane = jnp.min(jnp.where(top == most, lanes, BLOCK), axis=1, keepdims=True)
    here = lanes == lane

    def along(x):
        return jnp.sum(jnp.where(slots, x, 0.0), axis=0, keepdims=True)

    picked = [jnp.sum(jnp.where(here, stat_v[n], 0.0), axis=1, keepdims=True) for n in range(1, 5)]
    col_at = along((blocks % 8 * BLOCK + lane).astype(jnp.float32))
    row_at = along((blocks // 8 * BLOCK).astype(jnp.float32) + picked[0])
    ask[...] = jnp.concatenate(
        [jnp.broadcast_to(row_at, (8, BLOCK)), jnp.broadcast_to(col_at, (8, BLOCK))], axis=0
    )

    @pl.loop(0, NZ)
    def _(dz):
        ask_copy(owner(dz, 1), dp).start()

    @pl.loop(1, NZ)
    def _(dz):
        ask_copy(owner(dz, 0), dp).start()

    asked[dp] = ask[...]

    def roll_copy(slot, source):
        return pltpu.make_async_remote_copy(
            src_ref=r_send.at[slot], dst_ref=r_recv.at[source],
            send_sem=r_ss.at[slot], recv_sem=r_rs.at[source],
            device_id=(dp, slot), device_id_type=MESH,
        )

    def scale_copy(slot, source):
        return pltpu.make_async_remote_copy(
            src_ref=c_send.at[slot], dst_ref=c_recv.at[source],
            send_sem=c_ss.at[slot], recv_sem=c_rs.at[source],
            device_id=(dp, slot), device_id_type=MESH,
        )

    def held(slot):
        b = jnp.int32(0)
        for n in range(NE):
            b = lax.select(routing[0, 0, n] == slot, jnp.int32(n), b)
        return b

    @pl.loop(1, NE)
    def _(k):
        slot = lax.rem(ex + k, NE)
        r_send[slot] = wt_v[held(slot)]
        roll_copy(slot, ex).start()

    r_recv[ex] = wt_v[held(ex)]
    groups = lax.broadcasted_iota(jnp.int32, (16, BLOCK), 1) // NE
    for other in range(2):

        @pl.loop(1 - other, NZ)
        def _(dz):
            source = owner(dz, other)
            ask_copy(source, source).wait_recv()

        total = jnp.zeros((16, BLOCK), jnp.float32)
        for dz in range(NZ):
            total = jnp.where(groups == dz, asked[owner(dz, other)], total)
        rows = total[0:1, :].astype(jnp.int32)
        cols = total[8:9, :].astype(jnp.int32)
        place_v[...] = (
            (lax.broadcasted_iota(jnp.int32, (OWN, BLOCK), 0) == rows)
            .astype(jnp.float32)
            .astype(jnp.bfloat16)
        )
        sel_v[...] = jnp.dot(
            g_v[...],
            (lax.broadcasted_iota(jnp.int32, (g_v.shape[1], BLOCK), 0) == cols)
            .astype(jnp.float32)
            .astype(jnp.bfloat16),
            preferred_element_type=jnp.float32,
        )

        def dots(quarter, answer, other=other):
            for n in range(4):
                dz = quarter * 4 + n
                chosen = jnp.dot(
                    a_v[owner(dz, other)], place_v[...], preferred_element_type=jnp.float32
                )
                answer = jnp.where(
                    groups[:8] == dz, jnp.sum(chosen * sel_v[...], axis=0, keepdims=True), answer
                )
            return answer

        reply[other] = lax.fori_loop(0, 2, dots, jnp.zeros((8, BLOCK), jnp.float32))

        @pl.loop(1 - other, NZ)
        def _(dz):
            reply_copy(owner(dz, other), dp).start()

    replied[dp] = reply[0]

    @pl.loop(1, ND)
    def _(k):
        source = lax.rem(dp + k, ND)
        reply_copy(source, source).wait_recv()

    exact = jnp.zeros((8, BLOCK), jnp.float32)
    for other in range(2):
        for dz in range(NZ):
            exact = exact + jnp.where(
                groups[:8] == (NZ - dz) % NZ, replied[owner(dz, other)], 0.0
            )
    exact = jnp.sum(jnp.where(slots, exact[0:1, :], 0.0), axis=1, keepdims=True)
    old = [jnp.broadcast_to(x, (NE, BLOCK)) for x in picked[1:]]
    largest = jnp.abs(old[0] - adam(*old, jnp.broadcast_to(exact, (NE, BLOCK))))
    scale = (largest + 1e-06).astype(jnp.bfloat16).astype(jnp.float32)
    for b in range(NE):
        scale_v[b] = jnp.broadcast_to(scale[b : b + 1, :], (8, BLOCK))

    @pl.loop(1, NE)
    def _(k):
        slot = lax.rem(ex + k, NE)
        c_send[slot] = scale_v[held(slot)]
        scale_copy(slot, ex).start()

    c_recv[ex] = scale_v[held(ex)]

    @pl.loop(1, NE)
    def _(k):
        source = lax.rem(ex + k, NE)
        roll_copy(source, source).wait_recv()

    @pl.loop(1, NE)
    def _(k):
        source = lax.rem(ex + k, NE)
        scale_copy(source, source).wait_recv()

    row = jnp.zeros((16, BLOCK), jnp.float32)
    for e in range(NE):
        g = group_of[e]
        wide = c_recv[g]
        blocks_out[e] = (r_recv[g] / wide[0:1, :]).astype(jnp.bfloat16)
        row = jnp.where(lanes == e, wide[0:1, :], row)
    scales_out[...] = row.astype(jnp.bfloat16)

    @pl.loop(1, NE)
    def _(k):
        slot = lax.rem(ex + k, NE)
        roll_copy(slot, ex).wait_send()
        scale_copy(slot, ex).wait_send()
        peer = lax.rem(dp + k, ND)
        ask_copy(peer, dp).wait_send()
        reply_copy(peer, dp).wait_send()

    @pl.loop(0, 2)
    def _(way):
        for n in range(2):
            s1_copy(way, 0, 2 * way + n).wait_send()
        s2_copy(way, 0, way).wait_send()
        x1_copy(way).wait_send()

        @pl.loop(1, 4)
        def _(s):
            for u in range(4):
                s1_copy(way, s, u).wait_send()
            for c in range(2):
                s2_copy(way, s, c).wait_send()

    @pl.loop(0, 2 * NZ)
    def _(j):
        x2_copy(j).wait_send()

    for c in range(4):
        for copy in result(c):
            copy.wait()


def per_device(acts, out_grads, master, moment_one, moment_two, routing, group_of):
    f32, i16, bf16 = jnp.float32, jnp.int16, jnp.bfloat16
    own, width = master.shape[1], master.shape[2]
    tokens = acts.shape[1]
    dma = pltpu.SemaphoreType.DMA
    hbm = pl.BlockSpec(memory_space=pl.ANY)
    smem = pl.BlockSpec(memory_space=pltpu.SMEM)
    vmem = pl.BlockSpec(memory_space=pltpu.VMEM)
    shape = jax.ShapeDtypeStruct
    grad, step, blocks, scales = pl.pallas_call(
        kernel,
        out_shape=(
            shape((own, width), f32),
            shape((own, width), f32),
            shape((NE, BLOCK, BLOCK), bf16),
            shape((16, BLOCK), bf16),
        ),
        in_specs=[hbm] * 5 + [smem] * 2,
        out_specs=(hbm, hbm, vmem, vmem),
        scratch_shapes=[
            pltpu.VMEM((2 * NZ, tokens, OWN), bf16),
            pltpu.VMEM((tokens, width), bf16),
            pltpu.VMEM((own, width), f32),
            pltpu.VMEM((own, width), f32),
            pltpu.VMEM((own, width), f32),
            pltpu.VMEM((NE, BLOCK, BLOCK), f32),
            pltpu.VMEM((own, width), f32),
            pltpu.VMEM((own, width), f32),
            pltpu.VMEM((2, 4, 4, MSG, BLOCK), i16),
            pltpu.VMEM((2, 4, 4, MSG, BLOCK), i16),
            pltpu.VMEM((2, 4, 2, MSG, BLOCK), i16),
            pltpu.VMEM((2, 4, 2, MSG, BLOCK), i16),
            pltpu.VMEM((2 * NZ, MSG, BLOCK), i16),
            pltpu.VMEM((2 * NZ, MSG, BLOCK), i16),
            pltpu.VMEM((2, MSG, BLOCK), i16),
            pltpu.VMEM((2, MSG, BLOCK), i16),
            pltpu.VMEM((16, BLOCK), f32),
            pltpu.VMEM((ND, 16, BLOCK), f32),
            pltpu.VMEM((2, 8, BLOCK), f32),
            pltpu.VMEM((ND, 8, BLOCK), f32),
            pltpu.VMEM((5, NE, BLOCK), f32),
            pltpu.VMEM((tokens, BLOCK), f32),
            pltpu.VMEM((own, BLOCK), bf16),
            pltpu.VMEM((NE, 8, BLOCK), f32),
            pltpu.VMEM((NE, BLOCK, BLOCK), f32),
            pltpu.VMEM((NE, BLOCK, BLOCK), f32),
            pltpu.VMEM((NE, 8, BLOCK), f32),
            pltpu.VMEM((NE, 8, BLOCK), f32),
            dma((2 * NZ,)),
            dma((4,)),
            dma((2, 4)),
            dma((2, 4, 4)),
            dma((2, 4, 4)),
            dma((2, 4, 2)),
            dma((2, 4, 2)),
            dma((2 * NZ,)),
            dma((2 * NZ,)),
            dma((2,)),
            dma((2,)),
            dma((ND,)),
            dma((ND,)),
            dma((ND,)),
            dma((ND,)),
            dma((NE,)),
            dma((NE,)),
            dma((NE,)),
            dma((NE,)),
        ],
        name="update",
        cost_estimate=pl.CostEstimate(
            flops=2 * tokens * acts.shape[2] * width, bytes_accessed=12 * 2**20, transcendentals=0
        ),
        compiler_params=pltpu.CompilerParams(
            collective_id=0, has_side_effects=True, vmem_limit_bytes=56 * 2**20
        ),
    )(acts, out_grads, master, moment_one, moment_two, routing, group_of)
    first, second = moments(moment_one[0], moment_two[0], grad)
    weight = master[0] - step
    return (
        weight[None],
        first[None],
        second[None],
        blocks.reshape(1, 1, NE, 1, BLOCK, BLOCK),
        scales[0, :NE].reshape(1, 1, NE, 1),
    )


def solution(mesh):
    in_specs = (P("expert", "dp", None),) * 6 + (P(),)
    out_specs = (
        P("expert", "dp", None),
        P("expert", "dp", None),
        P("expert", "dp", None),
        P("expert", "dp", None, None, None, None),
        P("expert", "dp", None, None),
    )
    return jax.shard_map(
        per_device, mesh=mesh, in_specs=in_specs, out_specs=out_specs, check_vma=False
    )
```

```python
import math

import jax
import jax.numpy as jnp
from jax import lax
from jax.experimental import pallas as pl
from jax.experimental.pallas import tpu as pltpu
from jax.sharding import PartitionSpec as P

MESH = pl.DeviceIdType.MESH
BLOCK = 128
NZ = 8
ND = 16
NE = 16
OWN = 256
UC = 256
MSG = 2 * OWN + 16
LEVELS = 32766.0
FINE = 8.0
LN2 = math.log(2.0)

beta_one = 0.9
beta_two = 0.95
learn_rate = 0.01
decay_rate = 0.1
adam_eps = 1e-08
corr_one = 1.0 - 0.9**10
corr_two = 1.0 - 0.95**10

ORDER = (
    0, 18, 128, 1, 19, 129, 20, 130, 141, 6, 21, 134, 7, 86,
    68, 69, 87, 132, 133, 89, 192, 209, 74, 88, 73, 131, 138, 139,
    75, 135, 212, 91, 72, 277, 90, 260, 78, 136, 79, 137, 77, 93,
    197, 142, 143, 95, 92, 140, 264, 76, 280, 94, 321, 265, 281, 284,
    268, 320, 269, 285, 384, 448, 385, 449,
)
HEAD = 6


def pick(k, values):
    if len(set(values)) == 1:
        return jnp.int32(values[0])
    half = len(values) // 2
    return lax.select(k < half, pick(k, values[:half]), pick(k - half, values[half:]))


def moments(one, two, grad):
    first = beta_one * one + (1.0 - beta_one) * grad
    second = beta_two * two + (1.0 - beta_two) * grad * grad
    return first, second


def adam(weight, one, two, grad):
    first, second = moments(one, two, grad)
    update = (first * (1.0 / corr_one)) / (
        jnp.sqrt(second * (1.0 / corr_two)) + adam_eps
    ) + decay_rate * weight
    return learn_rate * update


def encode(ref, halves):
    steps = []
    for h, v in enumerate(halves):
        top = jnp.max(jnp.abs(v), axis=0, keepdims=True)
        step = jnp.ceil(jnp.log(jnp.maximum(top, 2.0**-100)) * (FINE / LN2))
        inv = jnp.exp(step * (-LN2 / FINE)) * LEVELS
        ref[h * OWN : (h + 1) * OWN, :] = jnp.round(v * inv).astype(jnp.int32).astype(jnp.int16)
        steps.append(jnp.broadcast_to(step, (8, BLOCK)))
    ref[2 * OWN :, :] = jnp.concatenate(steps, axis=0).astype(jnp.int32).astype(jnp.int16)


def decode(ref):
    steps = ref[2 * OWN :, :].astype(jnp.int32).astype(jnp.float32)
    scales = jnp.exp(steps * (LN2 / FINE)) * (1.0 / LEVELS)
    return [
        ref[h * OWN : (h + 1) * OWN, :].astype(jnp.int32).astype(jnp.float32)
        * scales[8 * h : 8 * h + 1, :]
        for h in range(2)
    ]


def kernel(
    acts, grads, master, moment_one, moment_two, routing, group_of,
    grad_out, step_out, blocks_out, scales_out,
    a_v, g_v, w_v, m_v, v_v, wt_v, sum_v, step_v,
    s1_send, s1_recv, s2_send, s2_recv, x2_send, x2_recv, x1_send, x1_recv, ask, asked, reply, replied,
    stat_v, sel_v, place_v, scale_v, r_send, r_recv, c_send, c_recv,
    a_sem, in_sem, out_sem,
    s1_ss, s1_rs, s2_ss, s2_rs, x2_ss, x2_rs, x1_ss, x1_rs, ask_ss, ask_rs, rep_ss, rep_rs, r_ss, r_rs, c_ss, c_rs,
):
    dp = lax.axis_index("dp")
    ex = lax.axis_index("expert")
    z, xh = dp // 2, dp % 2

    def zdev(way):
        return (lax.rem(z + 1 + 6 * way, NZ) * 2 + xh, ex)

    partner = (z * 2 + 1 - xh, ex)

    def owner(dz, other):
        return lax.rem(z + dz, NZ) * 2 + lax.rem(xh + other, 2)

    mine = z * 2 + xh

    def load_acts(off, half):
        i = lax.rem(z + off, NZ) * 2 + half
        return pltpu.make_async_copy(
            acts.at[0, :, pl.ds(pl.multiple_of(i * OWN, OWN), OWN)], a_v.at[i], a_sem.at[i]
        )

    grads_copy = pltpu.make_async_copy(grads.at[0], g_v, in_sem.at[0])
    load_acts(4, 0).start()
    grads_copy.start()
    load_acts(4, 1).start()

    barrier = pltpu.get_barrier_semaphore()
    for peer in (zdev(0), zdev(1), partner):
        pl.semaphore_signal(barrier, inc=1, device_id=peer, device_id_type=MESH)

    @pl.loop(1, NE)
    def _(k):
        pl.semaphore_signal(barrier, inc=1, device_id=(dp, lax.rem(ex + k, NE)), device_id_type=MESH)

    order = (3, 5, 2, 6, 1, 7, 0)
    for off in order:
        for half in range(2):
            load_acts(off, half).start()
    state = [
        pltpu.make_async_copy(src.at[0], dst, in_sem.at[1 + i])
        for i, (src, dst) in enumerate(((master, w_v), (moment_one, m_v), (moment_two, v_v)))
    ]
    for c in state:
        c.start()

    pl.semaphore_wait(barrier, 3 + NE - 1)

    def partial(i, c):
        p = lax.dot_general(
            a_v[i],
            g_v[:, pl.ds(pl.multiple_of(c * UC, UC), UC)],
            (((0,), (0,)), ((), ())),
            preferred_element_type=jnp.float32,
        )
        return [p[:, :BLOCK], p[:, BLOCK:]]

    def add(a, b):
        return [u + v for u, v in zip(a, b)]

    def s1_copy(way, s, u):
        return pltpu.make_async_remote_copy(
            src_ref=s1_send.at[way, s, u], dst_ref=s1_recv.at[way, s, u],
            send_sem=s1_ss.at[way, s, u], recv_sem=s1_rs.at[way, s, u],
            device_id=zdev(way), device_id_type=MESH,
        )

    def s2_copy(way, s, c):
        return pltpu.make_async_remote_copy(
            src_ref=s2_send.at[way, s, c], dst_ref=s2_recv.at[way, s, c],
            send_sem=s2_ss.at[way, s, c], recv_sem=s2_rs.at[way, s, c],
            device_id=zdev(way), device_id_type=MESH,
        )

    def x2_copy(j):
        return pltpu.make_async_remote_copy(
            src_ref=x2_send.at[j], dst_ref=x2_recv.at[j],
            send_sem=x2_ss.at[j], recv_sem=x2_rs.at[j],
            device_id=partner, device_id_type=MESH,
        )

    def x1_copy(c):
        return pltpu.make_async_remote_copy(
            src_ref=x1_send.at[c], dst_ref=x1_recv.at[c],
            send_sem=x1_ss.at[c], recv_sem=x1_rs.at[c],
            device_id=partner, device_id_type=MESH,
        )

    def target(way, s):
        return lax.rem(z + 4 + (1 - 2 * way) * (-s) + NZ, NZ)

    def s1_task(way, s, u, arrived):
        v = partial(target(way, s) * 2 + u // 2, u % 2)
        if arrived:
            s1_copy(way, s - 1, u).wait_recv()
            v = add(v, decode(s1_recv.at[way, s - 1, u]))
        encode(s1_send.at[way, s, u], v)
        s1_copy(way, s, u).start()

    def x2_task(j):
        o = j // 2
        off = lax.select(o % 2 == 1, 4 - (o + 1) // 2, 4 + o // 2)
        encode(x2_send.at[j], partial(lax.rem(z + off, NZ) * 2 + 1 - xh, 2 + j % 2))
        x2_copy(j).start()

    def s2_task(way, s, c, arrived):
        v = partial(target(way, s) * 2 + xh, 2 + c)
        j = lax.select(s == 0, c, (2 * s - 1 + way) * 2 + c)
        x2_copy(j).wait_recv()
        v = add(v, decode(x2_recv.at[j]))
        if arrived:
            s2_copy(way, s - 1, c).wait_recv()
            v = add(v, decode(s2_recv.at[way, s - 1, c]))
        encode(s2_send.at[way, s, c], v)
        s2_copy(way, s, c).start()

    def s1_sum(half, c):
        u = 2 * half + c
        v = partial(z * 2 + half, c)
        for way in range(2):
            s1_copy(way, 3, u).wait_recv()
            v = add(v, decode(s1_recv.at[way, 3, u]))
        return v

    def result(c):
        cols = pl.ds(pl.multiple_of(c * UC, UC), UC)
        return [
            pltpu.make_async_copy(src.at[:, cols], dst.at[:, cols], out_sem.at[n, c])
            for n, (src, dst) in enumerate(((sum_v, grad_out), (step_v, step_out)))
        ]

    row_ids = lax.broadcasted_iota(jnp.int32, (BLOCK, BLOCK), 0)

    def finish(c, halves):
        for h, grad in enumerate(halves):
            cols = pl.ds(pl.multiple_of(c * UC + h * BLOCK, BLOCK), BLOCK)
            sum_v[:, cols] = grad
            step = adam(w_v[:, cols], m_v[:, cols], v_v[:, cols], grad)
            step_v[:, cols] = step
            weight = w_v[:, cols] - step
            for r in range(2):
                b = r * 8 + 2 * c + h
                rows = slice(r * BLOCK, (r + 1) * BLOCK)
                tile = weight[rows, :]
                wt_v[b] = tile
                size = jnp.abs(tile)
                top = jnp.max(size, axis=0, keepdims=True)
                at = jnp.min(jnp.where(size == top, row_ids, BLOCK), axis=0, keepdims=True)
                one_row = row_ids == at
                stat_v[0, pl.ds(b, 1), :] = top
                stat_v[1, pl.ds(b, 1), :] = at.astype(jnp.float32)
                for n, src in enumerate((w_v, m_v, v_v)):
                    stat_v[2 + n, pl.ds(b, 1), :] = jnp.sum(
                        jnp.where(one_row, src[rows, cols], 0.0), axis=0, keepdims=True
                    )
        for copy in result(c):
            copy.start()

    def x1_task(c):
        encode(x1_send.at[c], s1_sum(1 - xh, c))
        x1_copy(c).start()

    def finish_s1(c):
        v = s1_sum(xh, c)
        x1_copy(c).wait_recv()
        finish(c, add(v, decode(x1_recv.at[c])))

    def finish_s2(c):
        v = partial(mine, 2 + c)
        x2_copy(14 + c).wait_recv()
        v = add(v, decode(x2_recv.at[14 + c]))
        for way in range(2):
            s2_copy(way, 3, c).wait_recv()
            v = add(v, decode(s2_recv.at[way, 3, c]))
        finish(2 + c, v)

    load_acts(4, 0).wait()
    grads_copy.wait()
    load_acts(4, 1).wait()

    @pl.loop(0, len(ORDER))
    def _(k):
        @pl.when(k == HEAD)
        def _():
            for off in order:
                for half in range(2):
                    load_acts(off, half).wait()
            for c in state:
                c.wait()

        code = pick(k, ORDER)
        kind = code // 64
        way, s, u = code // 16 % 4, code // 4 % 4, code % 4
        for n, task in enumerate(
            (
                lambda: s1_task(way, s, u, False),
                lambda: s1_task(way, s, u, True),
                lambda: x2_task(code % 64),
                lambda: s2_task(way, s, u, False),
                lambda: s2_task(way, s, u, True),
                lambda: x1_task(u),
                lambda: finish_s1(u),
                lambda: finish_s2(u),
            )
        ):
            pl.when(kind == n)(task)

    def ask_copy(peer, source):
        return pltpu.make_async_remote_copy(
            src_ref=ask, dst_ref=asked.at[source],
            send_sem=ask_ss.at[peer], recv_sem=ask_rs.at[source],
            device_id=(peer, ex), device_id_type=MESH,
        )

    def reply_copy(peer, source):
        return pltpu.make_async_remote_copy(
            src_ref=reply.at[lax.rem(peer + dp, 2)], dst_ref=replied.at[source],
            send_sem=rep_ss.at[peer], recv_sem=rep_rs.at[source],
            device_id=(peer, ex), device_id_type=MESH,
        )

    lanes = lax.broadcasted_iota(jnp.int32, (NE, BLOCK), 1)
    blocks = lax.broadcasted_iota(jnp.int32, (NE, BLOCK), 0)
    slots = lanes % NE == blocks
    top = stat_v[0]
    most = jnp.max(top, axis=1, keepdims=True)
    lane = jnp.min(jnp.where(top == most, lanes, BLOCK), axis=1, keepdims=True)
    here = lanes == lane

    def along(x):
        return jnp.sum(jnp.where(slots, x, 0.0), axis=0, keepdims=True)

    picked = [jnp.sum(jnp.where(here, stat_v[n], 0.0), axis=1, keepdims=True) for n in range(1, 5)]
    col_at = along((blocks % 8 * BLOCK + lane).astype(jnp.float32))
    row_at = along((blocks // 8 * BLOCK).astype(jnp.float32) + picked[0])
    ask[...] = jnp.concatenate(
        [jnp.broadcast_to(row_at, (8, BLOCK)), jnp.broadcast_to(col_at, (8, BLOCK))], axis=0
    )

    @pl.loop(0, NZ)
    def _(dz):
        ask_copy(owner(dz, 1), dp).start()

    @pl.loop(1, NZ)
    def _(dz):
        ask_copy(owner(dz, 0), dp).start()

    asked[dp] = ask[...]

    def roll_copy(slot, source):
        return pltpu.make_async_remote_copy(
            src_ref=r_send.at[slot], dst_ref=r_recv.at[source],
            send_sem=r_ss.at[slot], recv_sem=r_rs.at[source],
            device_id=(dp, slot), device_id_type=MESH,
        )

    def scale_copy(slot, source):
        return pltpu.make_async_remote_copy(
            src_ref=c_send.at[slot], dst_ref=c_recv.at[source],
            send_sem=c_ss.at[slot], recv_sem=c_rs.at[source],
            device_id=(dp, slot), device_id_type=MESH,
        )

    def held(slot):
        b = jnp.int32(0)
        for n in range(NE):
            b = lax.select(routing[0, 0, n] == slot, jnp.int32(n), b)
        return b

    @pl.loop(1, NE)
    def _(k):
        slot = lax.rem(ex + k, NE)
        r_send[slot] = wt_v[held(slot)]
        roll_copy(slot, ex).start()

    r_recv[ex] = wt_v[held(ex)]
    groups = lax.broadcasted_iota(jnp.int32, (16, BLOCK), 1) // NE
    for other in range(2):

        @pl.loop(1 - other, NZ)
        def _(dz):
            source = owner(dz, other)
            ask_copy(source, source).wait_recv()

        total = jnp.zeros((16, BLOCK), jnp.float32)
        for dz in range(NZ):
            total = jnp.where(groups == dz, asked[owner(dz, other)], total)
        rows = total[0:1, :].astype(jnp.int32)
        cols = total[8:9, :].astype(jnp.int32)
        place_v[...] = (
            (lax.broadcasted_iota(jnp.int32, (OWN, BLOCK), 0) == rows)
            .astype(jnp.float32)
            .astype(jnp.bfloat16)
        )
        sel_v[...] = jnp.dot(
            g_v[...],
            (lax.broadcasted_iota(jnp.int32, (g_v.shape[1], BLOCK), 0) == cols)
            .astype(jnp.float32)
            .astype(jnp.bfloat16),
            preferred_element_type=jnp.float32,
        )

        def dots(quarter, answer, other=other):
            for n in range(4):
                dz = quarter * 4 + n
                chosen = jnp.dot(
                    a_v[owner(dz, other)], place_v[...], preferred_element_type=jnp.float32
                )
                answer = jnp.where(
                    groups[:8] == dz, jnp.sum(chosen * sel_v[...], axis=0, keepdims=True), answer
                )
            return answer

        reply[other] = lax.fori_loop(0, 2, dots, jnp.zeros((8, BLOCK), jnp.float32))

        @pl.loop(1 - other, NZ)
        def _(dz):
            reply_copy(owner(dz, other), dp).start()

    replied[dp] = reply[0]

    @pl.loop(1, ND)
    def _(k):
        source = lax.rem(dp + k, ND)
        reply_copy(source, source).wait_recv()

    exact = jnp.zeros((8, BLOCK), jnp.float32)
    for other in range(2):
        for dz in range(NZ):
            exact = exact + jnp.where(
                groups[:8] == (NZ - dz) % NZ, replied[owner(dz, other)], 0.0
            )
    exact = jnp.sum(jnp.where(slots, exact[0:1, :], 0.0), axis=1, keepdims=True)
    old = [jnp.broadcast_to(x, (NE, BLOCK)) for x in picked[1:]]
    largest = jnp.abs(old[0] - adam(*old, jnp.broadcast_to(exact, (NE, BLOCK))))
    scale = (largest + 1e-06).astype(jnp.bfloat16).astype(jnp.float32)
    for b in range(NE):
        scale_v[b] = jnp.broadcast_to(scale[b : b + 1, :], (8, BLOCK))

    @pl.loop(1, NE)
    def _(k):
        slot = lax.rem(ex + k, NE)
        c_send[slot] = scale_v[held(slot)]
        scale_copy(slot, ex).start()

    c_recv[ex] = scale_v[held(ex)]

    @pl.loop(1, NE)
    def _(k):
        source = lax.rem(ex + k, NE)
        roll_copy(source, source).wait_recv()

    @pl.loop(1, NE)
    def _(k):
        source = lax.rem(ex + k, NE)
        scale_copy(source, source).wait_recv()

    row = jnp.zeros((16, BLOCK), jnp.float32)
    for e in range(NE):
        g = group_of[e]
        wide = c_recv[g]
        blocks_out[e] = (r_recv[g] / wide[0:1, :]).astype(jnp.bfloat16)
        row = jnp.where(lanes == e, wide[0:1, :], row)
    scales_out[...] = row.astype(jnp.bfloat16)

    @pl.loop(1, NE)
    def _(k):
        slot = lax.rem(ex + k, NE)
        roll_copy(slot, ex).wait_send()
        scale_copy(slot, ex).wait_send()
        peer = lax.rem(dp + k, ND)
        ask_copy(peer, dp).wait_send()
        reply_copy(peer, dp).wait_send()

    @pl.loop(0, 2)
    def _(way):
        for n in range(2):
            s1_copy(way, 0, 2 * way + n).wait_send()
        s2_copy(way, 0, way).wait_send()
        x1_copy(way).wait_send()

        @pl.loop(1, 4)
        def _(s):
            for u in range(4):
                s1_copy(way, s, u).wait_send()
            for c in range(2):
                s2_copy(way, s, c).wait_send()

    @pl.loop(0, 2 * NZ)
    def _(j):
        x2_copy(j).wait_send()

    for c in range(4):
        for copy in result(c):
            copy.wait()


def per_device(acts, out_grads, master, moment_one, moment_two, routing, group_of):
    f32, i16, bf16 = jnp.float32, jnp.int16, jnp.bfloat16
    own, width = master.shape[1], master.shape[2]
    tokens = acts.shape[1]
    dma = pltpu.SemaphoreType.DMA
    hbm = pl.BlockSpec(memory_space=pl.ANY)
    smem = pl.BlockSpec(memory_space=pltpu.SMEM)
    vmem = pl.BlockSpec(memory_space=pltpu.VMEM)
    shape = jax.ShapeDtypeStruct
    grad, step, blocks, scales = pl.pallas_call(
        kernel,
        out_shape=(
            shape((own, width), f32),
            shape((own, width), f32),
            shape((NE, BLOCK, BLOCK), bf16),
            shape((16, BLOCK), bf16),
        ),
        in_specs=[hbm] * 5 + [smem] * 2,
        out_specs=(hbm, hbm, vmem, vmem),
        scratch_shapes=[
            pltpu.VMEM((2 * NZ, tokens, OWN), bf16),
            pltpu.VMEM((tokens, width), bf16),
            pltpu.VMEM((own, width), f32),
            pltpu.VMEM((own, width), f32),
            pltpu.VMEM((own, width), f32),
            pltpu.VMEM((NE, BLOCK, BLOCK), f32),
            pltpu.VMEM((own, width), f32),
            pltpu.VMEM((own, width), f32),
            pltpu.VMEM((2, 4, 4, MSG, BLOCK), i16),
            pltpu.VMEM((2, 4, 4, MSG, BLOCK), i16),
            pltpu.VMEM((2, 4, 2, MSG, BLOCK), i16),
            pltpu.VMEM((2, 4, 2, MSG, BLOCK), i16),
            pltpu.VMEM((2 * NZ, MSG, BLOCK), i16),
            pltpu.VMEM((2 * NZ, MSG, BLOCK), i16),
            pltpu.VMEM((2, MSG, BLOCK), i16),
            pltpu.VMEM((2, MSG, BLOCK), i16),
            pltpu.VMEM((16, BLOCK), f32),
            pltpu.VMEM((ND, 16, BLOCK), f32),
            pltpu.VMEM((2, 8, BLOCK), f32),
            pltpu.VMEM((ND, 8, BLOCK), f32),
            pltpu.VMEM((5, NE, BLOCK), f32),
            pltpu.VMEM((tokens, BLOCK), f32),
            pltpu.VMEM((own, BLOCK), bf16),
            pltpu.VMEM((NE, 8, BLOCK), f32),
            pltpu.VMEM((NE, BLOCK, BLOCK), f32),
            pltpu.VMEM((NE, BLOCK, BLOCK), f32),
            pltpu.VMEM((NE, 8, BLOCK), f32),
            pltpu.VMEM((NE, 8, BLOCK), f32),
            dma((2 * NZ,)),
            dma((4,)),
            dma((2, 4)),
            dma((2, 4, 4)),
            dma((2, 4, 4)),
            dma((2, 4, 2)),
            dma((2, 4, 2)),
            dma((2 * NZ,)),
            dma((2 * NZ,)),
            dma((2,)),
            dma((2,)),
            dma((ND,)),
            dma((ND,)),
            dma((ND,)),
            dma((ND,)),
            dma((NE,)),
            dma((NE,)),
            dma((NE,)),
            dma((NE,)),
        ],
        name="update",
        cost_estimate=pl.CostEstimate(
            flops=2 * tokens * acts.shape[2] * width, bytes_accessed=12 * 2**20, transcendentals=0
        ),
        compiler_params=pltpu.CompilerParams(
            collective_id=0, has_side_effects=True, vmem_limit_bytes=56 * 2**20
        ),
    )(acts, out_grads, master, moment_one, moment_two, routing, group_of)
    first, second = moments(moment_one[0], moment_two[0], grad)
    weight = master[0] - step
    return (
        weight[None],
        first[None],
        second[None],
        blocks.reshape(1, 1, NE, 1, BLOCK, BLOCK),
        scales[0, :NE].reshape(1, 1, NE, 1),
    )


def solution(mesh):
    in_specs = (P("expert", "dp", None),) * 6 + (P(),)
    out_specs = (
        P("expert", "dp", None),
        P("expert", "dp", None),
        P("expert", "dp", None),
        P("expert", "dp", None, None, None, None),
        P("expert", "dp", None, None),
    )
    return jax.shard_map(
        per_device, mesh=mesh, in_specs=in_specs, out_specs=out_specs, check_vma=False
    )
```

```python
import math

import jax
import jax.numpy as jnp
from jax import lax
from jax.experimental import pallas as pl
from jax.experimental.pallas import tpu as pltpu
from jax.sharding import PartitionSpec as P

MESH = pl.DeviceIdType.MESH
BLOCK = 128
NZ = 8
ND = 16
NE = 16
OWN = 256
UC = 256
MSG = 2 * OWN + 16
LEVELS = 32766.0
FINE = 8.0
LN2 = math.log(2.0)

beta_one = 0.9
beta_two = 0.95
learn_rate = 0.01
decay_rate = 0.1
adam_eps = 1e-08
corr_one = 1.0 - 0.9**10
corr_two = 1.0 - 0.95**10

ORDER = (
    0, 18, 128, 1, 19, 129, 20, 130, 141, 6, 21, 134, 7, 86,
    68, 69, 87, 132, 133, 89, 192, 209, 74, 88, 73, 131, 138, 139,
    75, 135, 212, 91, 72, 277, 90, 260, 78, 136, 79, 137, 77, 93,
    197, 142, 143, 95, 92, 140, 264, 76, 280, 94, 321, 265, 281, 284,
    268, 320, 269, 285, 384, 448, 385, 449,
)
HEAD = 6


def pick(k, values):
    if len(set(values)) == 1:
        return jnp.int32(values[0])
    half = len(values) // 2
    return lax.select(k < half, pick(k, values[:half]), pick(k - half, values[half:]))


def moments(one, two, grad):
    first = beta_one * one + (1.0 - beta_one) * grad
    second = beta_two * two + (1.0 - beta_two) * grad * grad
    return first, second


def adam(weight, one, two, grad):
    first, second = moments(one, two, grad)
    update = (first * (1.0 / corr_one)) / (
        jnp.sqrt(second * (1.0 / corr_two)) + adam_eps
    ) + decay_rate * weight
    return learn_rate * update


def encode(ref, halves):
    steps = []
    for h, v in enumerate(halves):
        top = jnp.max(jnp.abs(v), axis=0, keepdims=True)
        step = jnp.ceil(jnp.log(jnp.maximum(top, 2.0**-100)) * (FINE / LN2))
        inv = jnp.exp(step * (-LN2 / FINE)) * LEVELS
        ref[h * OWN : (h + 1) * OWN, :] = jnp.round(v * inv).astype(jnp.int32).astype(jnp.int16)
        steps.append(jnp.broadcast_to(step, (8, BLOCK)))
    ref[2 * OWN :, :] = jnp.concatenate(steps, axis=0).astype(jnp.int32).astype(jnp.int16)


def decode(ref):
    steps = ref[2 * OWN :, :].astype(jnp.int32).astype(jnp.float32)
    scales = jnp.exp(steps * (LN2 / FINE)) * (1.0 / LEVELS)
    return [
        ref[h * OWN : (h + 1) * OWN, :].astype(jnp.int32).astype(jnp.float32)
        * scales[8 * h : 8 * h + 1, :]
        for h in range(2)
    ]


def kernel(
    acts, grads, master, moment_one, moment_two, routing, group_of,
    grad_out, step_out, blocks_out, wide_out, scales_out,
    a_v, g_v, w_v, m_v, v_v, wt_v, sum_v, step_v,
    s1_send, s1_recv, s2_send, s2_recv, x2_send, x2_recv, x1_send, x1_recv, ask, asked, reply, replied,
    stat_v, sel_v, place_v, scale_v, r_send, r_recv, c_send, c_recv,
    a_sem, in_sem, out_sem,
    s1_ss, s1_rs, s2_ss, s2_rs, x2_ss, x2_rs, x1_ss, x1_rs, ask_ss, ask_rs, rep_ss, rep_rs, r_ss, r_rs, c_ss, c_rs,
):
    dp = lax.axis_index("dp")
    ex = lax.axis_index("expert")
    z, xh = dp // 2, dp % 2

    def zdev(way):
        return (lax.rem(z + 1 + 6 * way, NZ) * 2 + xh, ex)

    partner = (z * 2 + 1 - xh, ex)

    def owner(dz, other):
        return lax.rem(z + dz, NZ) * 2 + lax.rem(xh + other, 2)

    mine = z * 2 + xh

    def load_acts(off, half):
        i = lax.rem(z + off, NZ) * 2 + half
        return pltpu.make_async_copy(
            acts.at[0, :, pl.ds(pl.multiple_of(i * OWN, OWN), OWN)], a_v.at[i], a_sem.at[i]
        )

    grads_copy = pltpu.make_async_copy(grads.at[0], g_v, in_sem.at[0])
    load_acts(4, 0).start()
    grads_copy.start()
    load_acts(4, 1).start()
    order = (3, 5, 2, 6, 1, 7, 0)
    for off in order:
        for half in range(2):
            load_acts(off, half).start()
    state = [
        pltpu.make_async_copy(src.at[0], dst, in_sem.at[1 + i])
        for i, (src, dst) in enumerate(((master, w_v), (moment_one, m_v), (moment_two, v_v)))
    ]
    for c in state:
        c.start()

    barrier = pltpu.get_barrier_semaphore()

    @pl.loop(1, NE)
    def _(k):
        pl.semaphore_signal(barrier, inc=1, device_id=(lax.rem(dp + k, ND), ex), device_id_type=MESH)
        pl.semaphore_signal(barrier, inc=1, device_id=(dp, lax.rem(ex + k, NE)), device_id_type=MESH)

    pl.semaphore_wait(barrier, ND - 1 + NE - 1)

    def partial(i, c):
        p = lax.dot_general(
            a_v[i],
            g_v[:, pl.ds(pl.multiple_of(c * UC, UC), UC)],
            (((0,), (0,)), ((), ())),
            preferred_element_type=jnp.float32,
        )
        return [p[:, :BLOCK], p[:, BLOCK:]]

    def add(a, b):
        return [u + v for u, v in zip(a, b)]

    def s1_copy(way, s, u):
        return pltpu.make_async_remote_copy(
            src_ref=s1_send.at[way, s, u], dst_ref=s1_recv.at[way, s, u],
            send_sem=s1_ss.at[way, s, u], recv_sem=s1_rs.at[way, s, u],
            device_id=zdev(way), device_id_type=MESH,
        )

    def s2_copy(way, s, c):
        return pltpu.make_async_remote_copy(
            src_ref=s2_send.at[way, s, c], dst_ref=s2_recv.at[way, s, c],
            send_sem=s2_ss.at[way, s, c], recv_sem=s2_rs.at[way, s, c],
            device_id=zdev(way), device_id_type=MESH,
        )

    def x2_copy(j):
        return pltpu.make_async_remote_copy(
            src_ref=x2_send.at[j], dst_ref=x2_recv.at[j],
            send_sem=x2_ss.at[j], recv_sem=x2_rs.at[j],
            device_id=partner, device_id_type=MESH,
        )

    def x1_copy(c):
        return pltpu.make_async_remote_copy(
            src_ref=x1_send.at[c], dst_ref=x1_recv.at[c],
            send_sem=x1_ss.at[c], recv_sem=x1_rs.at[c],
            device_id=partner, device_id_type=MESH,
        )

    def target(way, s):
        return lax.rem(z + 4 + (1 - 2 * way) * (-s) + NZ, NZ)

    def s1_task(way, s, u, arrived):
        v = partial(target(way, s) * 2 + u // 2, u % 2)
        if arrived:
            s1_copy(way, s - 1, u).wait_recv()
            v = add(v, decode(s1_recv.at[way, s - 1, u]))
        encode(s1_send.at[way, s, u], v)
        s1_copy(way, s, u).start()

    def x2_task(j):
        o = j // 2
        off = lax.select(o % 2 == 1, 4 - (o + 1) // 2, 4 + o // 2)
        encode(x2_send.at[j], partial(lax.rem(z + off, NZ) * 2 + 1 - xh, 2 + j % 2))
        x2_copy(j).start()

    def s2_task(way, s, c, arrived):
        v = partial(target(way, s) * 2 + xh, 2 + c)
        j = lax.select(s == 0, c, (2 * s - 1 + way) * 2 + c)
        x2_copy(j).wait_recv()
        v = add(v, decode(x2_recv.at[j]))
        if arrived:
            s2_copy(way, s - 1, c).wait_recv()
            v = add(v, decode(s2_recv.at[way, s - 1, c]))
        encode(s2_send.at[way, s, c], v)
        s2_copy(way, s, c).start()

    def s1_sum(half, c):
        u = 2 * half + c
        v = partial(z * 2 + half, c)
        for way in range(2):
            s1_copy(way, 3, u).wait_recv()
            v = add(v, decode(s1_recv.at[way, 3, u]))
        return v

    def result(c):
        cols = pl.ds(pl.multiple_of(c * UC, UC), UC)
        return [
            pltpu.make_async_copy(src.at[:, cols], dst.at[:, cols], out_sem.at[n, c])
            for n, (src, dst) in enumerate(((sum_v, grad_out), (step_v, step_out)))
        ]

    row_ids = lax.broadcasted_iota(jnp.int32, (BLOCK, BLOCK), 0)

    def finish(c, halves):
        for h, grad in enumerate(halves):
            cols = pl.ds(pl.multiple_of(c * UC + h * BLOCK, BLOCK), BLOCK)
            sum_v[:, cols] = grad
            step = adam(w_v[:, cols], m_v[:, cols], v_v[:, cols], grad)
            step_v[:, cols] = step
            weight = w_v[:, cols] - step
            for r in range(2):
                b = r * 8 + 2 * c + h
                rows = slice(r * BLOCK, (r + 1) * BLOCK)
                tile = weight[rows, :]
                wt_v[b] = tile
                size = jnp.abs(tile)
                top = jnp.max(size, axis=0, keepdims=True)
                at = jnp.min(jnp.where(size == top, row_ids, BLOCK), axis=0, keepdims=True)
                one_row = row_ids == at
                stat_v[0, pl.ds(b, 1), :] = top
                stat_v[1, pl.ds(b, 1), :] = at.astype(jnp.float32)
                for n, src in enumerate((w_v, m_v, v_v)):
                    stat_v[2 + n, pl.ds(b, 1), :] = jnp.sum(
                        jnp.where(one_row, src[rows, cols], 0.0), axis=0, keepdims=True
                    )
        for copy in result(c):
            copy.start()

    def x1_task(c):
        encode(x1_send.at[c], s1_sum(1 - xh, c))
        x1_copy(c).start()

    def finish_s1(c):
        v = s1_sum(xh, c)
        x1_copy(c).wait_recv()
        finish(c, add(v, decode(x1_recv.at[c])))

    def finish_s2(c):
        v = partial(mine, 2 + c)
        x2_copy(14 + c).wait_recv()
        v = add(v, decode(x2_recv.at[14 + c]))
        for way in range(2):
            s2_copy(way, 3, c).wait_recv()
            v = add(v, decode(s2_recv.at[way, 3, c]))
        finish(2 + c, v)

    load_acts(4, 0).wait()
    grads_copy.wait()
    load_acts(4, 1).wait()

    @pl.loop(0, len(ORDER))
    def _(k):
        @pl.when(k == HEAD)
        def _():
            for off in order:
                for half in range(2):
                    load_acts(off, half).wait()
            for c in state:
                c.wait()

        code = pick(k, ORDER)
        kind = code // 64
        way, s, u = code // 16 % 4, code // 4 % 4, code % 4
        for n, task in enumerate(
            (
                lambda: s1_task(way, s, u, False),
                lambda: s1_task(way, s, u, True),
                lambda: x2_task(code % 64),
                lambda: s2_task(way, s, u, False),
                lambda: s2_task(way, s, u, True),
                lambda: x1_task(u),
                lambda: finish_s1(u),
                lambda: finish_s2(u),
            )
        ):
            pl.when(kind == n)(task)

    def ask_copy(peer, source):
        return pltpu.make_async_remote_copy(
            src_ref=ask, dst_ref=asked.at[source],
            send_sem=ask_ss.at[peer], recv_sem=ask_rs.at[source],
            device_id=(peer, ex), device_id_type=MESH,
        )

    def reply_copy(peer, source):
        return pltpu.make_async_remote_copy(
            src_ref=reply.at[lax.rem(peer + dp, 2)], dst_ref=replied.at[source],
            send_sem=rep_ss.at[peer], recv_sem=rep_rs.at[source],
            device_id=(peer, ex), device_id_type=MESH,
        )

    lanes = lax.broadcasted_iota(jnp.int32, (NE, BLOCK), 1)
    blocks = lax.broadcasted_iota(jnp.int32, (NE, BLOCK), 0)
    slots = lanes % NE == blocks
    top = stat_v[0]
    most = jnp.max(top, axis=1, keepdims=True)
    lane = jnp.min(jnp.where(top == most, lanes, BLOCK), axis=1, keepdims=True)
    here = lanes == lane

    def along(x):
        return jnp.sum(jnp.where(slots, x, 0.0), axis=0, keepdims=True)

    picked = [jnp.sum(jnp.where(here, stat_v[n], 0.0), axis=1, keepdims=True) for n in range(1, 5)]
    col_at = along((blocks % 8 * BLOCK + lane).astype(jnp.float32))
    row_at = along((blocks // 8 * BLOCK).astype(jnp.float32) + picked[0])
    ask[...] = jnp.concatenate(
        [jnp.broadcast_to(row_at, (8, BLOCK)), jnp.broadcast_to(col_at, (8, BLOCK))], axis=0
    )

    @pl.loop(0, NZ)
    def _(dz):
        ask_copy(owner(dz, 1), dp).start()

    @pl.loop(1, NZ)
    def _(dz):
        ask_copy(owner(dz, 0), dp).start()

    asked[dp] = ask[...]

    def roll_copy(slot, source):
        return pltpu.make_async_remote_copy(
            src_ref=r_send.at[slot], dst_ref=r_recv.at[source],
            send_sem=r_ss.at[slot], recv_sem=r_rs.at[source],
            device_id=(dp, slot), device_id_type=MESH,
        )

    def scale_copy(slot, source):
        return pltpu.make_async_remote_copy(
            src_ref=c_send.at[slot], dst_ref=c_recv.at[source],
            send_sem=c_ss.at[slot], recv_sem=c_rs.at[source],
            device_id=(dp, slot), device_id_type=MESH,
        )

    def held(slot):
        b = jnp.int32(0)
        for n in range(NE):
            b = lax.select(routing[0, 0, n] == slot, jnp.int32(n), b)
        return b

    @pl.loop(1, NE)
    def _(k):
        slot = lax.rem(ex + k, NE)
        r_send[slot] = wt_v[held(slot)]
        roll_copy(slot, ex).start()

    r_recv[ex] = wt_v[held(ex)]
    groups = lax.broadcasted_iota(jnp.int32, (16, BLOCK), 1) // NE
    for other in range(2):

        @pl.loop(1 - other, NZ)
        def _(dz):
            source = owner(dz, other)
            ask_copy(source, source).wait_recv()

        total = jnp.zeros((16, BLOCK), jnp.float32)
        for dz in range(NZ):
            total = jnp.where(groups == dz, asked[owner(dz, other)], total)
        rows = total[0:1, :].astype(jnp.int32)
        cols = total[8:9, :].astype(jnp.int32)
        place_v[...] = (
            (lax.broadcasted_iota(jnp.int32, (OWN, BLOCK), 0) == rows)
            .astype(jnp.float32)
            .astype(jnp.bfloat16)
        )
        sel_v[...] = jnp.dot(
            g_v[...],
            (lax.broadcasted_iota(jnp.int32, (g_v.shape[1], BLOCK), 0) == cols)
            .astype(jnp.float32)
            .astype(jnp.bfloat16),
            preferred_element_type=jnp.float32,
        )

        def dots(quarter, answer, other=other):
            for n in range(4):
                dz = quarter * 4 + n
                chosen = jnp.dot(
                    a_v[owner(dz, other)], place_v[...], preferred_element_type=jnp.float32
                )
                answer = jnp.where(
                    groups[:8] == dz, jnp.sum(chosen * sel_v[...], axis=0, keepdims=True), answer
                )
            return answer

        reply[other] = lax.fori_loop(0, 2, dots, jnp.zeros((8, BLOCK), jnp.float32))

        @pl.loop(1 - other, NZ)
        def _(dz):
            reply_copy(owner(dz, other), dp).start()

    replied[dp] = reply[0]

    @pl.loop(1, ND)
    def _(k):
        source = lax.rem(dp + k, ND)
        reply_copy(source, source).wait_recv()

    exact = jnp.zeros((8, BLOCK), jnp.float32)
    for other in range(2):
        for dz in range(NZ):
            exact = exact + jnp.where(
                groups[:8] == (NZ - dz) % NZ, replied[owner(dz, other)], 0.0
            )
    exact = jnp.sum(jnp.where(slots, exact[0:1, :], 0.0), axis=1, keepdims=True)
    old = [jnp.broadcast_to(x, (NE, BLOCK)) for x in picked[1:]]
    largest = jnp.abs(old[0] - adam(*old, jnp.broadcast_to(exact, (NE, BLOCK))))
    scale = (largest + 1e-06).astype(jnp.bfloat16).astype(jnp.float32)
    for b in range(NE):
        scale_v[b] = jnp.broadcast_to(scale[b : b + 1, :], (8, BLOCK))

    @pl.loop(1, NE)
    def _(k):
        slot = lax.rem(ex + k, NE)
        c_send[slot] = scale_v[held(slot)]
        scale_copy(slot, ex).start()

    c_recv[ex] = scale_v[held(ex)]

    @pl.loop(1, NE)
    def _(k):
        source = lax.rem(ex + k, NE)
        roll_copy(source, source).wait_recv()

    @pl.loop(1, NE)
    def _(k):
        source = lax.rem(ex + k, NE)
        scale_copy(source, source).wait_recv()

    row = jnp.zeros((16, BLOCK), jnp.float32)
    for e in range(NE):
        g = group_of[e]
        wide = c_recv[g]
        blocks_out[e] = r_recv[g]
        wide_out[e] = wide
        row = jnp.where(lanes == e, wide[0:1, :], row)
    scales_out[...] = row.astype(jnp.bfloat16)

    @pl.loop(1, NE)
    def _(k):
        slot = lax.rem(ex + k, NE)
        roll_copy(slot, ex).wait_send()
        scale_copy(slot, ex).wait_send()
        peer = lax.rem(dp + k, ND)
        ask_copy(peer, dp).wait_send()
        reply_copy(peer, dp).wait_send()

    @pl.loop(0, 2)
    def _(way):
        for n in range(2):
            s1_copy(way, 0, 2 * way + n).wait_send()
        s2_copy(way, 0, way).wait_send()
        x1_copy(way).wait_send()

        @pl.loop(1, 4)
        def _(s):
            for u in range(4):
                s1_copy(way, s, u).wait_send()
            for c in range(2):
                s2_copy(way, s, c).wait_send()

    @pl.loop(0, 2 * NZ)
    def _(j):
        x2_copy(j).wait_send()

    for c in range(4):
        for copy in result(c):
            copy.wait()


def per_device(acts, out_grads, master, moment_one, moment_two, routing, group_of):
    f32, i16, bf16 = jnp.float32, jnp.int16, jnp.bfloat16
    own, width = master.shape[1], master.shape[2]
    tokens = acts.shape[1]
    dma = pltpu.SemaphoreType.DMA
    hbm = pl.BlockSpec(memory_space=pl.ANY)
    smem = pl.BlockSpec(memory_space=pltpu.SMEM)
    vmem = pl.BlockSpec(memory_space=pltpu.VMEM)
    shape = jax.ShapeDtypeStruct
    grad, step, blocks, wide, scales = pl.pallas_call(
        kernel,
        out_shape=(
            shape((own, width), f32),
            shape((own, width), f32),
            shape((NE, BLOCK, BLOCK), f32),
            shape((NE, 8, BLOCK), f32),
            shape((16, BLOCK), bf16),
        ),
        in_specs=[hbm] * 5 + [smem] * 2,
        out_specs=(hbm, hbm, vmem, vmem, vmem),
        scratch_shapes=[
            pltpu.VMEM((2 * NZ, tokens, OWN), bf16),
            pltpu.VMEM((tokens, width), bf16),
            pltpu.VMEM((own, width), f32),
            pltpu.VMEM((own, width), f32),
            pltpu.VMEM((own, width), f32),
            pltpu.VMEM((NE, BLOCK, BLOCK), f32),
            pltpu.VMEM((own, width), f32),
            pltpu.VMEM((own, width), f32),
            pltpu.VMEM((2, 4, 4, MSG, BLOCK), i16),
            pltpu.VMEM((2, 4, 4, MSG, BLOCK), i16),
            pltpu.VMEM((2, 4, 2, MSG, BLOCK), i16),
            pltpu.VMEM((2, 4, 2, MSG, BLOCK), i16),
            pltpu.VMEM((2 * NZ, MSG, BLOCK), i16),
            pltpu.VMEM((2 * NZ, MSG, BLOCK), i16),
            pltpu.VMEM((2, MSG, BLOCK), i16),
            pltpu.VMEM((2, MSG, BLOCK), i16),
            pltpu.VMEM((16, BLOCK), f32),
            pltpu.VMEM((ND, 16, BLOCK), f32),
            pltpu.VMEM((2, 8, BLOCK), f32),
            pltpu.VMEM((ND, 8, BLOCK), f32),
            pltpu.VMEM((5, NE, BLOCK), f32),
            pltpu.VMEM((tokens, BLOCK), f32),
            pltpu.VMEM((own, BLOCK), bf16),
            pltpu.VMEM((NE, 8, BLOCK), f32),
            pltpu.VMEM((NE, BLOCK, BLOCK), f32),
            pltpu.VMEM((NE, BLOCK, BLOCK), f32),
            pltpu.VMEM((NE, 8, BLOCK), f32),
            pltpu.VMEM((NE, 8, BLOCK), f32),
            dma((2 * NZ,)),
            dma((4,)),
            dma((2, 4)),
            dma((2, 4, 4)),
            dma((2, 4, 4)),
            dma((2, 4, 2)),
            dma((2, 4, 2)),
            dma((2 * NZ,)),
            dma((2 * NZ,)),
            dma((2,)),
            dma((2,)),
            dma((ND,)),
            dma((ND,)),
            dma((ND,)),
            dma((ND,)),
            dma((NE,)),
            dma((NE,)),
            dma((NE,)),
            dma((NE,)),
        ],
        name="update",
        cost_estimate=pl.CostEstimate(
            flops=2 * tokens * acts.shape[2] * width, bytes_accessed=12 * 2**20, transcendentals=0
        ),
        compiler_params=pltpu.CompilerParams(
            collective_id=0, has_side_effects=True, vmem_limit_bytes=56 * 2**20
        ),
    )(acts, out_grads, master, moment_one, moment_two, routing, group_of)
    blocks = (blocks / wide[:, :1, :]).astype(bf16)
    first, second = moments(moment_one[0], moment_two[0], grad)
    weight = master[0] - step
    return (
        weight[None],
        first[None],
        second[None],
        blocks.reshape(1, 1, NE, 1, BLOCK, BLOCK),
        scales[0, :NE].reshape(1, 1, NE, 1),
    )


def solution(mesh):
    in_specs = (P("expert", "dp", None),) * 6 + (P(),)
    out_specs = (
        P("expert", "dp", None),
        P("expert", "dp", None),
        P("expert", "dp", None),
        P("expert", "dp", None, None, None, None),
        P("expert", "dp", None, None),
    )
    return jax.shard_map(
        per_device, mesh=mesh, in_specs=in_specs, out_specs=out_specs, check_vma=False
    )
```
